512 devices in a mesh: gx: 8 (over x, z_hi), gy: 4 (over y), gz: 16 (over z_lo, core).
Axes of the slice: x: 4, y: 4, z: 16 (z_hi: 2, z_lo: 8; z = z_hi * 8 + z_lo), core: 2. Of those that a mesh axis runs over, the one named last changes fastest.
Arguments:
- volume: float32 [128, 128, 1024], P('gz', 'gx', 'gy'), may hold values from -10 to 10
Outputs:
- diffused: float32 [128, 128, 1024], P('gz', 'gx', 'gy')
The draws below stay inside these ranges and needn't reach their ends.
All inputs are finite; a program needn't handle non-finite values.
Results may differ from the reference program's by a relative error of at most 0.0003.
Values sent between devices are 32-bit elements; how exact they have to be, the bound alone decides.
A program may use at most 64 MiB of HBM per device.

```python
import math
import jax
import jax.numpy as jnp
from jax import lax

CZ = 8
CX = 16
NZ = 128
NX = 128
NY = 1024


def smooth_field(key, term_count):
    keys = jax.random.split(key, 4)
    directions = jax.random.normal(keys[0], (term_count, 3), jnp.float32)
    directions = directions / jnp.sqrt(jnp.sum(directions * directions, axis=1, keepdims=True) + 1e-06)
    wavelengths = jax.random.uniform(keys[1], (term_count,), jnp.float32, 40.0, 160.0)
    phases = jax.random.uniform(keys[2], (term_count,), jnp.float32, 0.0, 2.0 * math.pi)
    weights = jax.random.normal(keys[3], (term_count,), jnp.float32)
    z_pos = jnp.arange(NZ, dtype=jnp.float32)[:, None, None]
    x_pos = jnp.arange(NX, dtype=jnp.float32)[None, :, None]
    y_pos = jnp.arange(NY, dtype=jnp.float32)[None, None, :]
    field = jnp.zeros((NZ, NX, NY), jnp.float32)
    for term in range(term_count):
        rate = 2.0 * math.pi / wavelengths[term]
        angle = rate * (directions[term, 0] * z_pos + directions[term, 1] * x_pos + directions[term, 2] * y_pos) + phases[term]
        field = field + weights[term] * jnp.cos(angle)
    return field / math.sqrt(0.5 * term_count)


def draw_volume(key, part):
    keys = jax.random.split(key, 3)
    region = 1.5 * jnp.tanh(3.0 * smooth_field(keys[0], 6))
    loudness = 0.5 + 1.5 * jax.nn.sigmoid(2.0 * smooth_field(keys[1], 4))
    noise = jnp.clip(jax.random.normal(keys[2], (NZ, NX, NY), jnp.float32), -4.0, 4.0)
    values = region + loudness * noise
    return values.astype(jnp.float32)


def setup_inputs(seed: int = 0) -> dict:
    key_of = jax.random.split(jax.random.key(seed), 2)
    volume = draw_volume(jax.random.fold_in(key_of[1], 71), 0)
    return {"volume": volume}


kernel_taps = (0.41111229, 0.8007374, 1.0, 0.8007374, 0.41111229)
time_step = 3000.0
contrast = 0.1


def blur_valid(values, first_dim):
    weight_sum = sum(kernel_taps)
    for axis_dim in range(first_dim, first_dim + 3):
        out_size = values.shape[axis_dim] - 4
        blurred = (kernel_taps[0] / weight_sum) * lax.slice_in_dim(values, 0, out_size, axis=axis_dim)
        for offset in range(1, 5):
            blurred = blurred + (kernel_taps[offset] / weight_sum) * lax.slice_in_dim(values, offset, offset + out_size, axis=axis_dim)
        values = blurred
    return values


def gradients(values, first_dim):
    result = []
    for axis_dim in range(first_dim, first_dim + 3):
        cropped = values
        for other_dim in range(first_dim, first_dim + 3):
            if other_dim != axis_dim:
                cropped = lax.slice_in_dim(cropped, 1, cropped.shape[other_dim] - 1, axis=other_dim)
        length = cropped.shape[axis_dim] - 2
        forward = lax.slice_in_dim(cropped, 2, length + 2, axis=axis_dim)
        behind = lax.slice_in_dim(cropped, 0, length, axis=axis_dim)
        result.append((forward - behind) * 0.5)
    return result


def shifted(values, stride, axis_dim, fill_value):
    length = values.shape[axis_dim]
    if abs(stride) >= length:
        return jnp.full(values.shape, fill_value, values.dtype)
    pad_shape = list(values.shape)
    pad_shape[axis_dim] = abs(stride)
    padding = jnp.full(tuple(pad_shape), fill_value, values.dtype)
    if stride > 0:
        return jnp.concatenate([padding, lax.slice_in_dim(values, 0, length - stride, axis=axis_dim)], axis=axis_dim)
    return jnp.concatenate([lax.slice_in_dim(values, -stride, length, axis=axis_dim), padding], axis=axis_dim)


def every_other(values, first_row, axis_dim):
    return lax.slice_in_dim(values, first_row, values.shape[axis_dim], stride=2, axis=axis_dim)


def append_row(values, fill_value, axis_dim):
    row_shape = list(values.shape)
    row_shape[axis_dim] = 1
    return jnp.concatenate([values, jnp.full(tuple(row_shape), fill_value, values.dtype)], axis=axis_dim)


def reduce_solve(sub_diag, main_diag, super_diag, right_sides, axis_dim):
    length = main_diag.shape[axis_dim]
    if length == 1:
        return [right_side / main_diag for right_side in right_sides]
    if length % 2 == 1:
        sub_diag = append_row(sub_diag, 0.0, axis_dim)
        main_diag = append_row(main_diag, 1.0, axis_dim)
        super_diag = append_row(super_diag, 0.0, axis_dim)
        right_sides = [append_row(right_side, 0.0, axis_dim) for right_side in right_sides]
    even_sub = every_other(sub_diag, 0, axis_dim)
    odd_sub = every_other(sub_diag, 1, axis_dim)
    even_main = every_other(main_diag, 0, axis_dim)
    odd_main = every_other(main_diag, 1, axis_dim)
    even_super = every_other(super_diag, 0, axis_dim)
    odd_super = every_other(super_diag, 1, axis_dim)
    even_sides = [every_other(right_side, 0, axis_dim) for right_side in right_sides]
    odd_sides = [every_other(right_side, 1, axis_dim) for right_side in right_sides]
    lower_factor = -even_sub / shifted(odd_main, 1, axis_dim, 1.0)
    upper_factor = -even_super / odd_main
    reduced = reduce_solve(
        lower_factor * shifted(odd_sub, 1, axis_dim, 0.0),
        even_main + lower_factor * shifted(odd_super, 1, axis_dim, 0.0) + upper_factor * odd_sub,
        upper_factor * odd_super,
        [even_side + lower_factor * shifted(odd_side, 1, axis_dim, 0.0) + upper_factor * odd_side for even_side, odd_side in zip(even_sides, odd_sides)],
        axis_dim)
    result = []
    for even_part, odd_side in zip(reduced, odd_sides):
        odd_part = (odd_side - odd_sub * even_part - odd_super * shifted(even_part, -1, axis_dim, 0.0)) / odd_main
        joined = jnp.stack([even_part, odd_part], axis=axis_dim + 1)
        joined_shape = list(even_part.shape)
        joined_shape[axis_dim] = 2 * joined_shape[axis_dim]
        result.append(lax.slice_in_dim(joined.reshape(tuple(joined_shape)), 0, length, axis=axis_dim))
    return result


def inside_grid(squares, offsets, totals):
    full_shape = squares[0].shape
    inside_mask = None
    for axis_dim in range(3):
        global_index = offsets[axis_dim] + lax.broadcasted_iota(jnp.int32, full_shape, axis_dim)
        within = (global_index >= 0) & (global_index < totals[axis_dim])
        inside_mask = within if inside_mask is None else inside_mask & within
    return [jnp.where(inside_mask, square, 0.0) for square in squares]


def face_pairs(diffusivity, axis_dim, offset, total):
    cropped = diffusivity
    for other_dim in range(3):
        if other_dim != axis_dim:
            cropped = lax.slice_in_dim(cropped, 1, cropped.shape[other_dim] - 1, axis=other_dim)
    length = cropped.shape[axis_dim] - 2
    centre = lax.slice_in_dim(cropped, 1, length + 1, axis=axis_dim)
    following = lax.slice_in_dim(cropped, 2, length + 2, axis=axis_dim)
    before = lax.slice_in_dim(cropped, 0, length, axis=axis_dim)
    face_up = (centre + following) * 0.5
    face_down = (before + centre) * 0.5
    global_index = offset + lax.broadcasted_iota(jnp.int32, face_up.shape, axis_dim)
    face_up = jnp.where(global_index < total - 1, face_up, 0.0)
    face_down = jnp.where(global_index > 0, face_down, 0.0)
    return face_up, face_down


def line_system(values, face_up, face_down, axis_dim, stiffness):
    return reduce_solve(-stiffness * face_down, 1.0 + stiffness * (face_down + face_up), -stiffness * face_up, [values], axis_dim)[0]


def reference(volume):
    stiffness = 3.0 * time_step
    full_z, full_x, full_y = volume.shape
    padded = jnp.pad(volume, 6)

    def slab_work(slab_index):
        first_row = slab_index * CZ
        window = lax.dynamic_slice_in_dim(padded, first_row, CZ + 12, axis=0)
        blurred = blur_valid(window, 0)
        squares = inside_grid([slope * slope for slope in gradients(blurred, 0)], (first_row - 3, -3, -3), (full_z, full_x, full_y))
        diffusivity = [1.0 / (1.0 + blur_valid(square, 0) / (contrast * contrast)) for square in squares]
        up_z, down_z = face_pairs(diffusivity[0], 0, first_row, full_z)
        up_x, down_x = face_pairs(diffusivity[1], 1, 0, full_x)
        up_y, down_y = face_pairs(diffusivity[2], 2, 0, full_y)
        values = lax.dynamic_slice_in_dim(volume, first_row, CZ, axis=0)
        solved_x = line_system(values, up_x, down_x, 1, stiffness)
        solved_y = line_system(values, up_y, down_y, 2, stiffness)
        return solved_x + solved_y, up_z

    partial_sum, face_z = lax.map(slab_work, jnp.arange(full_z // CZ, dtype=jnp.int32))
    partial_sum = partial_sum.reshape((full_z, full_x, full_y))
    face_z = face_z.reshape((full_z, full_x, full_y))

    def column_work(slab_index):
        first_row = slab_index * CX
        values = lax.dynamic_slice_in_dim(volume, first_row, CX, axis=1)
        face_up = lax.dynamic_slice_in_dim(face_z, first_row, CX, axis=1)
        face_down = shifted(face_up, 1, 0, 0.0)
        return line_system(values, face_up, face_down, 0, stiffness)

    solved_z = lax.map(column_work, jnp.arange(full_x // CX, dtype=jnp.int32))
    solved_z = jnp.moveaxis(solved_z, 0, 1).reshape((full_z, full_x, full_y))
    return (partial_sum + solved_z) / 3.0
```

```python
import functools

import jax
import jax.numpy as jnp
from jax import lax
from jax.experimental import pallas as pl
from jax.experimental.pallas import tpu as pltpu
from jax.sharding import PartitionSpec as P

MESH = pl.DeviceIdType.MESH
F32 = jnp.float32
RAW_TAPS = (0.41111229, 0.8007374, 1.0, 0.8007374, 0.41111229)
TAPS = tuple(tap / sum(RAW_TAPS) for tap in RAW_TAPS)
STIFFNESS = 9000.0
CONTRAST = 0.1
NEAR = tuple((dz, dy) for dz in (-1, 0, 1) for dy in (-1, 0, 1) if dz or dy)
SOLVERS = 4
FIRST_SOLVER = 2


def roll_z(tile, j):
    return pltpu.roll(tile, (-j) % 8, tile.ndim - 2)


def roll_y(tile, j):
    return pltpu.roll(tile, (-j) % 128, tile.ndim - 1)


def taps_sum(parts):
    return TAPS[2] * parts[2] + TAPS[1] * (parts[1] + parts[3]) + TAPS[0] * (parts[0] + parts[4])


def ring_z(tiles, t, j, row):
    if j == 0:
        return tiles[t]
    if j > 0:
        return jnp.where(row < 8 - j, roll_z(tiles[t], j), roll_z(tiles[1 - t], j))
    return jnp.where(row >= -j, roll_z(tiles[t], j), roll_z(tiles[1 - t], j))


def ring_y(tiles, t, j, lane):
    if j == 0:
        return tiles[t]
    if j > 0:
        return jnp.where(lane < 128 - j, roll_y(tiles[t], j), roll_y(tiles[(t + 1) % 3], j))
    return jnp.where(lane >= -j, roll_y(tiles[t], j), roll_y(tiles[(t + 2) % 3], j))


def wide_z(down, own, up, row):
    inner, outer = [], []
    for j in range(-2, 3):
        if j == 0:
            inner.append(own)
            outer.append(jnp.where(row < 4, up, down))
            continue
        down_j, own_j, up_j = roll_z(down, j), roll_z(own, j), roll_z(up, j)
        if j > 0:
            inner.append(jnp.where(row < 8 - j, own_j, up_j))
            outer.append(jnp.where(row < 4, up_j, jnp.where(row < 8 - j, down_j, own_j)))
        else:
            inner.append(jnp.where(row >= -j, own_j, down_j))
            outer.append(jnp.where(row >= 4, down_j, jnp.where(row >= -j, up_j, own_j)))
    return taps_sum(inner), taps_sum(outer)


def reduce_block(count, get_face, get_value, keep):
    series = get_face(0)
    left_ground = jnp.ones_like(series)
    left_source = get_value(0)
    ground = jnp.ones_like(series)
    source = get_value(1)
    for j in range(1, count):
        face = get_face(j)
        inverse = 1.0 / (series + ground + face)
        to_left, to_next = series * inverse, face * inverse
        keep(j, to_left, to_next, source * inverse)
        left_ground = left_ground + to_left * ground
        left_source = left_source + to_left * source
        series = to_left * face
        if j < count - 1:
            ground = 1.0 + to_next * ground
            source = get_value(j + 1) + to_next * source
    return series, left_ground, to_next * ground, left_source, to_next * source


def merge_blocks(left, right):
    a_l, gl_l, gr_l, il_l, ir_l = left
    a_r, gl_r, gr_r, il_r, ir_r = right
    ground, source = gr_l + gl_r, ir_l + il_r
    inverse = 1.0 / (a_l + ground + a_r)
    to_l, to_r = a_l * inverse, a_r * inverse
    merged = (to_l * a_r, gl_l + to_l * ground, gr_r + to_r * ground, il_l + to_l * source, ir_r + to_r * source)
    return merged, (to_l, to_r, source * inverse)


def ladder_rings(series, ground, source, count, axis):
    size = series.shape[axis]
    step = 1
    while step < count:
        def low(array):
            return pltpu.roll(array, step, axis)

        def high(array):
            return pltpu.roll(array, size - step, axis)

        before = low(series)
        inverse = 1.0 / (ground + series + before)
        from_low, from_high = before * low(inverse), series * high(inverse)
        ground, source, series = (
            ground + from_low * low(ground) + from_high * high(ground),
            source + from_low * low(source) + from_high * high(source),
            from_high * high(series),
        )
        step *= 2
    return source / ground


def kernel(v_ref, o_ref, B, C, BL, SQ, GX, GZ, GY, XA, XOWN, XPEER, XG, SG, ZA, PZ, ZPEER, MS, ZR, RT, RV, SEP,
           GT, VT, YA, PY, YG, YS, XY, GIVE, ss_h, rs_h, ss_x, rs_x, ss_p, rs_p, ss_c, rs_c, ss_y, rs_y, ss_k, rs_k,
           ss_a, rs_a, ss_r, rs_r, ss_b, rs_b):
    gx, gy, gz = lax.axis_index("gx"), lax.axis_index("gy"), lax.axis_index("gz")
    zc, core = lax.div(gz, 2), lax.rem(gz, 2)
    xc, zh = lax.div(gx, 2), lax.rem(gx, 2)
    other_core = gz + 1 - 2 * core
    row = lax.broadcasted_iota(jnp.int32, (8, 128), 0)
    lane = lax.broadcasted_iota(jnp.int32, (8, 128), 1)

    def inside(dz, dy):
        z, y = gz + dz, gy + dy
        return jnp.logical_and(jnp.logical_and(z >= 0, z < 16), jnp.logical_and(y >= 0, y < 4))

    barrier = pltpu.get_barrier_semaphore()
    always = []
    for d in (2, 4, 6):
        always.append({"gx": lax.rem(gx + d, 8)})
    for d in (1, 2, 3):
        always.append({"gy": lax.rem(gy + d, 4)})
    for d in range(1, 8):
        always.append({"gz": lax.rem(zc + d, 8) * 2 + core})
    total = jnp.int32(len(always))

    @pl.when(gx > 0)
    def _():
        pl.semaphore_signal(barrier, inc=1, device_id={"gx": gx - 1}, device_id_type=MESH)

    @pl.when(gx < 7)
    def _():
        pl.semaphore_signal(barrier, inc=1, device_id={"gx": gx + 1}, device_id_type=MESH)

    total = total + jnp.where(gx > 0, 1, 0) + jnp.where(gx < 7, 1, 0)
    for target in always:
        pl.semaphore_signal(barrier, inc=1, device_id=target, device_id_type=MESH)
    for dz, dy in NEAR:
        total = total + jnp.where(inside(dz, dy), 1, 0)

        @pl.when(inside(dz, dy))
        def _():
            pl.semaphore_signal(barrier, inc=1, device_id={"gz": gz + dz, "gy": gy + dy}, device_id_type=MESH)

    for yt in range(2):
        XY[yt] = v_ref[:, 128 * yt:128 * yt + 128]
    for x in range(16):
        for yt in range(2):
            B[1, 1 + yt, x] = XY[yt, pl.ds(x, 8, stride=16), :]

    @pl.when(gz == 0)
    def _():
        B[0] = jnp.zeros((4, 27, 8, 128), F32)

    @pl.when(gz == 15)
    def _():
        B[2] = jnp.zeros((4, 27, 8, 128), F32)

    @pl.when(gy == 0)
    def _():
        for zt in range(3):
            B[zt, 0] = jnp.zeros((27, 8, 128), F32)

    @pl.when(gy == 3)
    def _():
        for zt in range(3):
            B[zt, 3] = jnp.zeros((27, 8, 128), F32)

    @pl.when(gx == 0)
    def _():
        for yt in (1, 2):
            B[1, yt, 22:27] = jnp.zeros((5, 8, 128), F32)

    @pl.when(gx == 7)
    def _():
        for yt in (1, 2):
            B[1, yt, 16:22] = jnp.zeros((6, 8, 128), F32)

    pl.semaphore_wait(barrier, total)

    def x_copy(i):
        if i == 0:
            source, target, device = B.at[1, 1:3, 0:6], B.at[1, 1:3, 16:22], {"gx": gx - 1}
        else:
            source, target, device = B.at[1, 1:3, 11:16], B.at[1, 1:3, 22:27], {"gx": gx + 1}
        return pltpu.make_async_remote_copy(
            src_ref=source, dst_ref=target, send_sem=ss_x.at[i], recv_sem=rs_x.at[i],
            device_id=device, device_id_type=MESH)

    @pl.when(gx > 0)
    def _():
        x_copy(0).start()

    @pl.when(gx < 7)
    def _():
        x_copy(1).start()

    def near_copy(phase, i):
        dz, dy = NEAR[i]
        xs = slice(0, 16) if phase == 0 else slice(16, 27)
        ys, yd = {0: (slice(1, 3), slice(1, 3)), 1: (slice(2, 3), slice(0, 1)), -1: (slice(1, 2), slice(3, 4))}[dy]
        return pltpu.make_async_remote_copy(
            src_ref=B.at[1, ys, xs], dst_ref=B.at[1 - dz, yd, xs],
            send_sem=ss_h.at[phase, i], recv_sem=rs_h.at[phase, i],
            device_id={"gz": gz + dz, "gy": gy + dy}, device_id_type=MESH)

    def near_start(phase):
        for i, (dz, dy) in enumerate(NEAR):
            @pl.when(inside(dz, dy))
            def _():
                near_copy(phase, i).start()

    def near_recv(phase):
        for i, (dz, dy) in enumerate(NEAR):
            @pl.when(inside(-dz, -dy))
            def _():
                near_copy(phase, i).wait_recv()

    def near_send(phase):
        for i, (dz, dy) in enumerate(NEAR):
            @pl.when(inside(dz, dy))
            def _():
                near_copy(phase, i).wait_send()

    near_start(0)

    def blur_zy(xi):
        columns = []
        for zt in range(3):
            halo = jnp.where(lane < 64, B[zt, 3, xi], B[zt, 0, xi])
            columns.append([B[zt, 1, xi], B[zt, 2, xi], halo])
        inner, outer = [], []
        for yt in range(3):
            a, b = wide_z(columns[0][yt], columns[1][yt], columns[2][yt], row)
            inner.append(a)
            outer.append(b)
        place = lax.rem(xi + 5, 27)
        for zt, tiles in enumerate((inner, outer)):
            for yt in range(3):
                C[place, zt, yt] = taps_sum([ring_y(tiles, yt, j, lane) for j in range(-2, 3)])

    def blur_loop(first, last):
        def step(xi, carry):
            blur_zy(xi)
            return carry
        lax.fori_loop(first, last, step, 0)

    near_recv(0)
    blur_loop(0, 16)

    @pl.when(gx < 7)
    def _():
        x_copy(0).wait_recv()

    @pl.when(gx > 0)
    def _():
        x_copy(1).wait_recv()

    near_start(1)
    near_recv(1)
    blur_loop(16, 27)

    def blur_x(p, carry):
        for zt in range(2):
            for yt in range(3):
                BL[p, zt, yt] = taps_sum([C[p + j, zt, yt] for j in range(5)])
        return carry
    lax.fori_loop(0, 23, blur_x, 0)

    above = jnp.where(gz < 15, 0.5, 0.0)
    below = jnp.where(gz > 0, 0.5, 0.0)
    right = jnp.where(gy < 3, 1.0, 0.0)
    left = jnp.where(gy > 0, 1.0, 0.0)
    z_half = (jnp.full((8, 128), 0.5, F32), jnp.where(row < 4, above, below).astype(F32))
    y_one = jnp.where(lane < 64, right, left).astype(F32)
    halves = [[z_half[0], z_half[0], z_half[0] * y_one], [z_half[1], z_half[1], z_half[1] * y_one]]

    def slopes(p, carry):
        x_in = jnp.where(jnp.logical_or(jnp.logical_and(p < 2, gx == 0), jnp.logical_and(p > 17, gx == 7)), 0.0, 1.0)
        tiles = [[BL[p + 1, zt, yt] for yt in range(3)] for zt in range(2)]
        for zt in range(2):
            for yt in range(3):
                half = halves[zt][yt] * x_in
                slope_x = (BL[p + 2, zt, yt] - BL[p, zt, yt]) * half
                SQ[0, p, zt, yt] = slope_x * slope_x
                column = [tiles[0][yt], tiles[1][yt]]
                slope_z = (ring_z(column, zt, 1, row) - ring_z(column, zt, -1, row)) * half
                SQ[1, p, zt, yt] = slope_z * slope_z
                slope_y = (ring_y(tiles[zt], yt, 1, lane) - ring_y(tiles[zt], yt, -1, lane)) * half
                SQ[2, p, zt, yt] = slope_y * slope_y
        return carry
    lax.fori_loop(0, 21, slopes, 0)

    def diffuse(tensor):
        return 1.0 / (1.0 + tensor * (1.0 / (CONTRAST * CONTRAST)))

    def tensor_x(a, p):
        return [[taps_sum([SQ[a, p + j, zt, yt] for j in range(5)]) for yt in range(3)] for zt in range(2)]

    def tensor_z(tiles, zt):
        return [taps_sum([ring_z([tiles[0][yt], tiles[1][yt]], zt, j, row) for j in range(-2, 3)]) for yt in range(3)]

    def tensor_y(tiles, yt):
        return taps_sum([ring_y(tiles, yt, j, lane) for j in range(-2, 3)])

    def face_x(p, before):
        tiles = tensor_z(tensor_x(0, p), 0)
        now = jnp.stack([diffuse(tensor_y(tiles, yt)) for yt in range(2)])
        scale = jnp.where(jnp.logical_and(p == 16, gx == 7), 0.0, 0.5 * STIFFNESS)

        @pl.when(p > 0)
        def _():
            GX[jnp.maximum(p - 1, 0)] = (before + now) * scale
        return now
    lax.fori_loop(0, 17, face_x, jnp.zeros((2, 8, 128), F32))

    def keep_x(j, to_left, to_next, source):
        XA[0, j], XA[1, j], XA[2, j] = to_left, to_next, source

    own_x = reduce_block(16, lambda j: GX[j], lambda j: B[1, 1:3, j], keep_x)
    for i in range(5):
        XOWN[i] = own_x[i]
    pair = pltpu.make_async_remote_copy(
        src_ref=XOWN, dst_ref=XPEER, send_sem=ss_p, recv_sem=rs_p,
        device_id={"gx": gx + 1 - 2 * zh}, device_id_type=MESH)
    pair.start()

    z_scale = jnp.where(jnp.logical_and(row == 7, gz == 15), 0.0, 0.5 * STIFFNESS).astype(F32)

    def face_z(p, carry):
        tiles = tensor_x(1, p)
        rows = [tensor_z(tiles, zt) for zt in range(2)]
        at = pl.multiple_of(p * 8, 8)
        for yt in range(2):
            own, halo = diffuse(tensor_y(rows[0], yt)), diffuse(tensor_y(rows[1], yt))
            GZ[yt, pl.ds(at, 8), :] = (own + ring_z([own, halo], 0, 1, row)) * z_scale
        return carry
    lax.fori_loop(0, 16, face_z, 0)

    def keep_z(j, to_left, to_next, source):
        ZA[0, j], ZA[1, j], ZA[2, j] = to_left, to_next, source

    def get_gz(j):
        return jnp.stack([GZ[yt, pl.ds(j, 16, stride=8), :] for yt in range(2)])

    def get_vz(j):
        return jnp.stack([v_ref[16 * j:16 * j + 16, 128 * yt:128 * yt + 128] for yt in range(2)])

    own_z = reduce_block(8, get_gz, get_vz, keep_z)
    for i in range(5):
        for h in range(2):
            PZ[h, i] = own_z[i][:, 8 * h:8 * h + 8, :]
    cores = pltpu.make_async_remote_copy(
        src_ref=PZ.at[1 - core], dst_ref=ZPEER, send_sem=ss_k, recv_sem=rs_k,
        device_id={"gz": other_core}, device_id_type=MESH)
    cores.start()

    y_scale = (jnp.full((8, 128), 0.5 * STIFFNESS, F32),
               jnp.where(jnp.logical_and(lane == 127, gy == 3), 0.0, 0.5 * STIFFNESS).astype(F32))

    def face_y(p, carry):
        tiles = tensor_z(tensor_x(2, p), 0)
        values = [diffuse(tensor_y(tiles, yt)) for yt in range(3)]
        at = pl.multiple_of(p * 8, 8)
        for yt in range(2):
            GY[yt, pl.ds(at, 8), :] = (values[yt] + ring_y(values, yt, 1, lane)) * y_scale[yt]
        return carry
    lax.fori_loop(0, 16, face_y, 0)

    cores.wait_recv()
    mine = [PZ[core, i] for i in range(5)]
    peer = [ZPEER[i] for i in range(5)]
    low = core == 0
    merged_z, middle_z = merge_blocks([jnp.where(low, a, b) for a, b in zip(mine, peer)],
                                      [jnp.where(low, b, a) for a, b in zip(mine, peer)])
    for i in range(5):
        for yt in range(2):
            MS[pl.ds(2 * i + yt, 8, stride=16), :] = merged_z[i][yt]

    def to_solver(k):
        return pltpu.make_async_remote_copy(
            src_ref=MS.at[pl.ds(32 * k, 32)], dst_ref=ZR.at[pl.ds(pl.multiple_of(zc * 32, 32), 32)],
            send_sem=ss_a.at[k], recv_sem=rs_a.at[zc],
            device_id={"gz": 2 * (FIRST_SOLVER + k) + core}, device_id_type=MESH)

    def from_chip(p):
        return pltpu.make_async_remote_copy(
            src_ref=MS.at[pl.ds(0, 32)], dst_ref=ZR.at[pl.ds(32 * p, 32)],
            send_sem=ss_a.at[0], recv_sem=rs_a.at[p],
            device_id={"gz": other_core}, device_id_type=MESH)

    for k in range(SOLVERS):
        @pl.when(zc != FIRST_SOLVER + k)
        def _():
            to_solver(k).start()

        @pl.when(zc == FIRST_SOLVER + k)
        def _():
            ZR[32 * (FIRST_SOLVER + k):32 * (FIRST_SOLVER + k) + 32, :] = MS[32 * k:32 * k + 32, :]

    for yt in range(2):
        GT[128 * yt:128 * yt + 128, :] = GY[yt].T
        VT[128 * yt:128 * yt + 128, :] = B[1, 1 + yt, 0:16].reshape(128, 128).T

    def keep_y(j, to_left, to_next, source):
        YA[0, j], YA[1, j], YA[2, j] = to_left, to_next, source

    own_y = reduce_block(32, lambda j: GT[pl.ds(j, 8, stride=32), :], lambda j: VT[pl.ds(j, 8, stride=32), :], keep_y)
    for i in range(5):
        PY[i] = own_y[i]

    def y_copy(d):
        return pltpu.make_async_remote_copy(
            src_ref=PY, dst_ref=YG.at[gy], send_sem=ss_y.at[d - 1], recv_sem=rs_y.at[d - 1],
            device_id={"gy": lax.rem(gy + d, 4)}, device_id_type=MESH)

    def y_back(d):
        return pltpu.make_async_remote_copy(
            src_ref=PY, dst_ref=YG.at[lax.rem(gy + 4 - d, 4)], send_sem=ss_y.at[d - 1], recv_sem=rs_y.at[d - 1],
            device_id={"gy": lax.rem(gy + d, 4)}, device_id_type=MESH)

    for d in (1, 2, 3):
        y_copy(d).start()
    YG[gy] = PY[...]

    is_solver = jnp.logical_and(zc >= FIRST_SOLVER, zc < FIRST_SOLVER + SOLVERS)
    place = jnp.clip(zc - FIRST_SOLVER, 0, SOLVERS - 1)

    def to_chip(p):
        return pltpu.make_async_remote_copy(
            src_ref=RT.at[pl.ds(8 * p, 8)], dst_ref=RV.at[pl.ds(pl.multiple_of(place * 8, 8), 8)],
            send_sem=ss_r.at[p], recv_sem=rs_r.at[place],
            device_id={"gz": 2 * p + core}, device_id_type=MESH)

    def from_solver(k):
        return pltpu.make_async_remote_copy(
            src_ref=RT.at[pl.ds(0, 8)], dst_ref=RV.at[pl.ds(8 * k, 8)],
            send_sem=ss_r.at[0], recv_sem=rs_r.at[k],
            device_id={"gz": other_core}, device_id_type=MESH)

    @pl.when(is_solver)
    def _():
        for p in range(8):
            @pl.when(zc != p)
            def _():
                from_chip(p).wait_recv()

        def gather(i):
            return jnp.stack([ZR[pl.ds(16 * rr + 2 * i + yt, 8, stride=32), :] for rr in range(2) for yt in range(2)])
        series, gl, gr, il, ir = [gather(i) for i in range(5)]
        sigma = ladder_rings(series, gl + pltpu.roll(gr, 1, 1), il + pltpu.roll(ir, 1, 1), 8, 1)
        following = pltpu.roll(sigma, 7, 1)
        for rr in range(2):
            for yt in range(2):
                RT[pl.ds(4 * rr + yt, 8, stride=8), :] = sigma[2 * rr + yt]
                RT[pl.ds(4 * rr + 2 + yt, 8, stride=8), :] = following[2 * rr + yt]
        for p in range(8):
            @pl.when(zc != p)
            def _():
                to_chip(p).start()

            @pl.when(zc == p)
            def _():
                RV[pl.ds(pl.multiple_of(place * 8, 8), 8), :] = RT[8 * p:8 * p + 8, :]

    for d in (1, 2, 3):
        y_back(d).wait_recv()
    series, gl, gr, il, ir = [YG[:, i].reshape(32, 128) for i in range(5)]
    sigma = ladder_rings(series, gl + pltpu.roll(gr, 1, 0), il + pltpu.roll(ir, 1, 0), 32, 0)
    YS[0] = sigma.reshape(4, 8, 128)
    YS[1] = pltpu.roll(sigma, 31, 0).reshape(4, 8, 128)
    first, solved = YS[0, gy], YS[1, gy]
    VT[pl.ds(0, 8, stride=32), :] = first
    for j in range(31, 0, -1):
        solved = YA[2, j] + YA[0, j] * first + YA[1, j] * solved
        VT[pl.ds(j, 8, stride=32), :] = solved
    for yt in range(2):
        XY[yt] = VT[128 * yt:128 * yt + 128, :].T

    pair.wait_recv()
    mine = [XOWN[i] for i in range(5)]
    peer = [XPEER[i] for i in range(5)]
    low_x = zh == 0
    merged_x, middle_x = merge_blocks([jnp.where(low_x, a, b) for a, b in zip(mine, peer)],
                                      [jnp.where(low_x, b, a) for a, b in zip(mine, peer)])
    for i in range(5):
        XG[xc, i] = merged_x[i]

    def xg_copy(d):
        return pltpu.make_async_remote_copy(
            src_ref=XG.at[xc], dst_ref=XG.at[xc], send_sem=ss_c.at[d - 1], recv_sem=rs_c.at[d - 1],
            device_id={"gx": lax.rem(gx + 2 * d, 8)}, device_id_type=MESH)

    def xg_back(d):
        return pltpu.make_async_remote_copy(
            src_ref=XG.at[xc], dst_ref=XG.at[lax.rem(xc + 4 - d, 4)], send_sem=ss_c.at[d - 1], recv_sem=rs_c.at[d - 1],
            device_id={"gx": lax.rem(gx + 2 * d, 8)}, device_id_type=MESH)

    for d in (1, 2, 3):
        xg_copy(d).start()

    for k in range(SOLVERS):
        @pl.when(zc != FIRST_SOLVER + k)
        def _():
            from_solver(k).wait_recv()

    def ends(w):
        return jnp.stack([RV[pl.ds(2 * w + yt, 8, stride=4), :] for yt in range(2)])
    start, end = ends(0), ends(1)
    middle = middle_z[2] + middle_z[0] * start + middle_z[1] * end
    SEP[core, 0] = jnp.where(low, start, middle)
    SEP[core, 1] = jnp.where(low, middle, end)
    GIVE[0] = jnp.where(low, middle, start)
    GIVE[1] = jnp.where(low, end, middle)
    give = pltpu.make_async_remote_copy(
        src_ref=GIVE, dst_ref=SEP.at[core], send_sem=ss_b, recv_sem=rs_b,
        device_id={"gz": other_core}, device_id_type=MESH)
    give.start()

    for d in (1, 2, 3):
        xg_back(d).wait_recv()
    ground, source = XG[0, 1], XG[0, 3]
    stack = []
    for p in range(4):
        series = XG[p, 0]
        inverse = 1.0 / (ground + series)
        ratio = series * inverse
        stack.append((source * inverse, ratio))
        if p < 3:
            ground = XG[p + 1, 1] + XG[p, 2] + ratio * ground
            source = XG[p + 1, 3] + XG[p, 4] + ratio * source
    value = stack[3][0]
    SG[4] = jnp.zeros((2, 8, 128), F32)
    SG[3] = value
    for p in (2, 1, 0):
        value = stack[p][0] + stack[p][1] * value
        SG[p] = value
    start_x, end_x = SG[xc], SG[xc + 1]
    middle_node = middle_x[2] + middle_x[0] * start_x + middle_x[1] * end_x
    first = jnp.where(low_x, start_x, middle_node)
    solved = jnp.where(low_x, middle_node, end_x)

    def add_x(j, value):
        for yt in range(2):
            XY[yt, 8 * j:8 * j + 8, :] = XY[yt, 8 * j:8 * j + 8, :] + value[yt]
    add_x(0, first)
    for j in range(15, 0, -1):
        solved = XA[2, j] + XA[0, j] * first + XA[1, j] * solved
        add_x(j, solved)

    pltpu.make_async_remote_copy(
        src_ref=GIVE, dst_ref=SEP.at[1 - core], send_sem=ss_b, recv_sem=rs_b,
        device_id={"gz": other_core}, device_id_type=MESH).wait_recv()
    first = jnp.concatenate([SEP[0, 0], SEP[1, 0]], axis=1)
    solved = jnp.concatenate([SEP[0, 1], SEP[1, 1]], axis=1)

    def write(j, value):
        for yt in range(2):
            o_ref[16 * j:16 * j + 16, 128 * yt:128 * yt + 128] = value[yt] + XY[yt, pl.ds(j, 16, stride=8), :]
    write(0, first)
    for j in range(7, 0, -1):
        solved = ZA[2, j] + ZA[0, j] * first + ZA[1, j] * solved
        write(j, solved)

    @pl.when(gx > 0)
    def _():
        x_copy(0).wait_send()

    @pl.when(gx < 7)
    def _():
        x_copy(1).wait_send()
    near_send(0)
    near_send(1)
    pair.wait_send()
    for d in (1, 2, 3):
        y_copy(d).wait_send()
        xg_copy(d).wait_send()
    for k in range(SOLVERS):
        @pl.when(zc != FIRST_SOLVER + k)
        def _():
            to_solver(k).wait_send()

    @pl.when(is_solver)
    def _():
        for p in range(8):
            @pl.when(zc != p)
            def _():
                to_chip(p).wait_send()
    cores.wait_send()
    give.wait_send()


def body(volume):
    tile = (8, 128)
    dma = pltpu.SemaphoreType.DMA
    vmem = [
        (3, 4, 27) + tile,
        (27, 2, 3) + tile,
        (23, 2, 3) + tile,
        (3, 21, 2, 3) + tile,
        (16, 2) + tile,
        (2, 128, 128),
        (2, 128, 128),
        (3, 16, 2) + tile,
        (5, 2) + tile,
        (5, 2) + tile,
        (4, 5, 2) + tile,
        (5, 2) + tile,
        (3, 8, 2, 16, 128),
        (2, 5, 2) + tile,
        (5, 2) + tile,
        (128, 128),
        (256, 128),
        (64, 128),
        (32, 128),
        (2, 2, 2) + tile,
        (256, 128),
        (256, 128),
        (3, 32) + tile,
        (5,) + tile,
        (4, 5) + tile,
        (2, 4) + tile,
        (2, 128, 128),
        (2, 2) + tile,
    ]
    sems = [(2, 8), (2, 8), (2,), (2,), None, None, (3,), (3,), (3,), (3,), None, None, (4,), (8,), (8,), (4,), None, None]
    total = pl.pallas_call(
        kernel,
        out_shape=jax.ShapeDtypeStruct((128, 256), F32),
        in_specs=[pl.BlockSpec(memory_space=pltpu.VMEM)],
        out_specs=pl.BlockSpec(memory_space=pltpu.VMEM),
        scratch_shapes=[pltpu.VMEM(shape, F32) for shape in vmem] + [dma(s) if s else dma for s in sems],
        compiler_params=pltpu.CompilerParams(
            collective_id=0, has_side_effects=True, vmem_limit_bytes=24 * 2**20),
        cost_estimate=pl.CostEstimate(flops=40_000_000, bytes_accessed=262144, transcendentals=0),
    )(volume.reshape(128, 256))
    return (total / 3.0).reshape(8, 16, 256)


def solution(mesh):
    return jax.shard_map(
        body,
        mesh=mesh,
        in_specs=(P("gz", "gx", "gy"),),
        out_specs=P("gz", "gx", "gy"),
        check_vma=False,
    )
```

```python
import functools

import jax
import jax.numpy as jnp
from jax import lax
from jax.experimental import pallas as pl
from jax.experimental.pallas import tpu as pltpu
from jax.sharding import PartitionSpec as P

MESH = pl.DeviceIdType.MESH
F32 = jnp.float32
RAW_TAPS = (0.41111229, 0.8007374, 1.0, 0.8007374, 0.41111229)
TAPS = tuple(tap / sum(RAW_TAPS) for tap in RAW_TAPS)
STIFFNESS = 9000.0
CONTRAST = 0.1
NEAR = tuple((dz, dy) for dz in (-1, 0, 1) for dy in (-1, 0, 1) if dz or dy)
SOLVERS = 4
FIRST_SOLVER = 2
U_BLUR, U_X, U_SLOPE, U_FACE = 2, 2, 2, 2


def roll_z(tile, j):
    return pltpu.roll(tile, (-j) % 8, tile.ndim - 2)


def roll_y(tile, j):
    return pltpu.roll(tile, (-j) % 128, tile.ndim - 1)


def taps_sum(parts):
    return TAPS[2] * parts[2] + TAPS[1] * (parts[1] + parts[3]) + TAPS[0] * (parts[0] + parts[4])


def ring_z(tiles, t, j, row):
    if j == 0:
        return tiles[t]
    if j > 0:
        return jnp.where(row < 8 - j, roll_z(tiles[t], j), roll_z(tiles[1 - t], j))
    return jnp.where(row >= -j, roll_z(tiles[t], j), roll_z(tiles[1 - t], j))


def ring_y(tiles, t, j, lane):
    if j == 0:
        return tiles[t]
    if j > 0:
        return jnp.where(lane < 128 - j, roll_y(tiles[t], j), roll_y(tiles[(t + 1) % 3], j))
    return jnp.where(lane >= -j, roll_y(tiles[t], j), roll_y(tiles[(t + 2) % 3], j))


def wide_z(down, own, up, row):
    inner, outer = [], []
    for j in range(-2, 3):
        if j == 0:
            inner.append(own)
            outer.append(jnp.where(row < 4, up, down))
            continue
        down_j, own_j, up_j = roll_z(down, j), roll_z(own, j), roll_z(up, j)
        if j > 0:
            inner.append(jnp.where(row < 8 - j, own_j, up_j))
            outer.append(jnp.where(row < 4, up_j, jnp.where(row < 8 - j, down_j, own_j)))
        else:
            inner.append(jnp.where(row >= -j, own_j, down_j))
            outer.append(jnp.where(row >= 4, down_j, jnp.where(row >= -j, up_j, own_j)))
    return taps_sum(inner), taps_sum(outer)


def loop(first, last, step, unroll):
    trips = (last - first) // unroll

    def some(t, carry):
        for u in range(unroll):
            step(first + t * unroll + u)
        return carry
    if trips:
        lax.fori_loop(0, trips, some, 0)
    for i in range(first + trips * unroll, last):
        step(i)


def reduce_block(count, get_face, get_value, keep):
    series = get_face(0)
    left_ground = jnp.ones_like(series)
    left_source = get_value(0)
    ground = jnp.ones_like(series)
    source = get_value(1)
    for j in range(1, count):
        face = get_face(j)
        inverse = 1.0 / (series + ground + face)
        to_left, to_next = series * inverse, face * inverse
        keep(j, to_left, to_next, source * inverse)
        left_ground = left_ground + to_left * ground
        left_source = left_source + to_left * source
        series = to_left * face
        if j < count - 1:
            ground = 1.0 + to_next * ground
            source = get_value(j + 1) + to_next * source
    return series, left_ground, to_next * ground, left_source, to_next * source


def merge_blocks(left, right):
    a_l, gl_l, gr_l, il_l, ir_l = left
    a_r, gl_r, gr_r, il_r, ir_r = right
    ground, source = gr_l + gl_r, ir_l + il_r
    inverse = 1.0 / (a_l + ground + a_r)
    to_l, to_r = a_l * inverse, a_r * inverse
    merged = (to_l * a_r, gl_l + to_l * ground, gr_r + to_r * ground, il_l + to_l * source, ir_r + to_r * source)
    return merged, (to_l, to_r, source * inverse)


def ladder_rings(series, ground, source, count, axis):
    size = series.shape[axis]
    step = 1
    while step < count:
        def low(array):
            return pltpu.roll(array, step, axis)

        def high(array):
            return pltpu.roll(array, size - step, axis)

        before = low(series)
        inverse = 1.0 / (ground + series + before)
        from_low, from_high = before * low(inverse), series * high(inverse)
        ground, source, series = (
            ground + from_low * low(ground) + from_high * high(ground),
            source + from_low * low(source) + from_high * high(source),
            from_high * high(series),
        )
        step *= 2
    return source / ground


def kernel(v_hbm, o_ref, v_ref, B, HS, HB, RB0, RB1, C, BL, SQ, GZ, GY, XA, XOWN, XPEER, XG, SG, ZA, PZ, ZPEER,
           MS, ZR, RT, RV, SEP, GT, VT, YA, PY, YG, YS, XY, GIVE, in_sem, ss_h, rs_h, ss_x, rs_x, ss_f, rs_f, ss_p, rs_p,
           ss_c, rs_c, ss_y, rs_y, ss_k, rs_k, ss_a, rs_a, ss_r, rs_r, ss_b, rs_b):
    gx, gy, gz = lax.axis_index("gx"), lax.axis_index("gy"), lax.axis_index("gz")
    zc, core = lax.div(gz, 2), lax.rem(gz, 2)
    xc, zh = lax.div(gx, 2), lax.rem(gx, 2)
    other_core = gz + 1 - 2 * core
    load = pltpu.make_async_copy(v_hbm, v_ref, in_sem)
    load.start()

    def chip_at(from_gx, dz):
        z = lax.rem(lax.rem(from_gx, 2) * 8 + zc + 16 + dz, 16)
        return lax.div(from_gx, 2) * 2 + lax.div(z, 8), lax.rem(z, 8) * 2 + core
    row = lax.broadcasted_iota(jnp.int32, (8, 128), 0)
    lane = lax.broadcasted_iota(jnp.int32, (8, 128), 1)

    def inside(dz, dy):
        z, y = gz + dz, gy + dy
        return jnp.logical_and(jnp.logical_and(z >= 0, z < 16), jnp.logical_and(y >= 0, y < 4))

    barrier = pltpu.get_barrier_semaphore()
    above_gx, above_gz = chip_at(gx, 4)
    below_gx, below_gz = chip_at(gx, -4)
    via_high = chip_at(gx + 1, 4)
    via_low = chip_at(jnp.maximum(gx - 1, 0), -4)
    always = [{"gx": above_gx, "gz": above_gz}, {"gx": below_gx, "gz": below_gz}]
    for d in (2, 4, 6):
        always.append({"gx": lax.rem(gx + d, 8)})
    for d in (1, 2, 3):
        always.append({"gy": lax.rem(gy + d, 4)})
    is_solver = jnp.logical_and(zc >= FIRST_SOLVER, zc < FIRST_SOLVER + SOLVERS)
    total = jnp.int32(len(always))

    @pl.when(gx < 7)
    def _():
        pl.semaphore_signal(barrier, inc=1, device_id={"gx": via_high[0], "gz": via_high[1]}, device_id_type=MESH)

    @pl.when(gx > 0)
    def _():
        pl.semaphore_signal(barrier, inc=1, device_id={"gx": via_low[0], "gz": via_low[1]}, device_id_type=MESH)

    total = total + jnp.where(below_gx > 0, 1, 0) + jnp.where(above_gx < 7, 1, 0)
    for target in always:
        pl.semaphore_signal(barrier, inc=1, device_id=target, device_id_type=MESH)
    for p in range(8):
        solves = FIRST_SOLVER <= p < FIRST_SOLVER + SOLVERS
        meets = zc != p if solves else is_solver
        total = total + jnp.where(meets, 1, 0)

        @pl.when(meets)
        def _():
            pl.semaphore_signal(barrier, inc=1, device_id={"gz": 2 * p + core}, device_id_type=MESH)
    for dz, dy in NEAR:
        total = total + jnp.where(inside(dz, dy), 1, 0)

        @pl.when(inside(dz, dy))
        def _():
            pl.semaphore_signal(barrier, inc=1, device_id={"gz": gz + dz, "gy": gy + dy}, device_id_type=MESH)

    def pack(phase, layers):
        low, high = None, None
        for i, x in enumerate(layers):
            a, b = B[1, 0, x], B[1, 1, x]
            a = pltpu.roll(a, 8 * i, 1) if i else a
            b = pltpu.roll(b, (8 * i + 8) % 128, 1) if i < 15 else b
            low = a if low is None else jnp.where(lane < 8 * i, low, a)
            high = b if high is None else jnp.where(lane < 8 * i, high, b)
        HS[0, phase], HS[1, phase] = low, high

    load.wait()
    for yt in range(2):
        XY[yt] = v_ref[:, 128 * yt:128 * yt + 128]
    for x in range(16):
        for yt in range(2):
            B[1, yt, x] = XY[yt, pl.ds(x, 8, stride=16), :]
    pack(0, range(16))

    @pl.when(gz == 0)
    def _():
        B[0] = jnp.zeros((2, 27, 8, 128), F32)
        HB[0] = jnp.zeros((2, 2, 8, 128), F32)

    @pl.when(gz == 15)
    def _():
        B[2] = jnp.zeros((2, 27, 8, 128), F32)
        HB[2] = jnp.zeros((2, 2, 8, 128), F32)

    @pl.when(gy == 0)
    def _():
        for zt in range(3):
            HB[zt, 0] = jnp.zeros((2, 8, 128), F32)

    @pl.when(gy == 3)
    def _():
        for zt in range(3):
            HB[zt, 1] = jnp.zeros((2, 8, 128), F32)

    @pl.when(gx == 0)
    def _():
        for yt in range(2):
            B[1, yt, 22:27] = jnp.zeros((5, 8, 128), F32)

    @pl.when(gx == 7)
    def _():
        for yt in range(2):
            B[1, yt, 16:22] = jnp.zeros((6, 8, 128), F32)

    pl.semaphore_wait(barrier, total)

    def x_first(i, yt):
        source, relay, device = ((B.at[1, yt, 0:6], RB0, {"gx": above_gx, "gz": above_gz}),
                                 (B.at[1, yt, 11:16], RB1, {"gx": below_gx, "gz": below_gz}))[i]
        return pltpu.make_async_remote_copy(
            src_ref=source, dst_ref=relay.at[yt], send_sem=ss_f.at[i, yt], recv_sem=rs_f.at[i, yt],
            device_id=device, device_id_type=MESH)

    def x_second(i, yt):
        relay, target, device = ((RB0, B.at[1, yt, 16:22], {"gx": below_gx - 1, "gz": below_gz}),
                                 (RB1, B.at[1, yt, 22:27], {"gx": above_gx + 1, "gz": above_gz}))[i]
        return pltpu.make_async_remote_copy(
            src_ref=relay.at[yt], dst_ref=target, send_sem=ss_x.at[i, yt], recv_sem=rs_x.at[i, yt],
            device_id=device, device_id_type=MESH)

    sends_x = (gx > 0, gx < 7)
    relays_x = (below_gx > 0, above_gx < 7)
    gets_x = (gx < 7, gx > 0)
    both = [(i, yt) for yt in range(2) for i in range(2)]

    for i, yt in both:
        @pl.when(sends_x[i])
        def _():
            x_first(i, yt).start()

    def near_copies(phase, i):
        dz, dy = NEAR[i]
        xs = slice(0, 16) if phase == 0 else slice(16, 27)
        if dy == 0:
            source, target = B.at[1, :, xs], B.at[1 - dz, :, xs]
        elif dy == 1:
            source, target = HS.at[1, phase], HB.at[1 - dz, 0, phase]
        else:
            source, target = HS.at[0, phase], HB.at[1 - dz, 1, phase]
        return pltpu.make_async_remote_copy(
            src_ref=source, dst_ref=target, send_sem=ss_h.at[phase, i], recv_sem=rs_h.at[phase, i],
            device_id={"gz": gz + dz, "gy": gy + dy}, device_id_type=MESH)

    def near_start(phase):
        for i, (dz, dy) in enumerate(NEAR):
            @pl.when(inside(dz, dy))
            def _():
                near_copies(phase, i).start()

    def near_recv(phase):
        for i, (dz, dy) in enumerate(NEAR):
            @pl.when(inside(-dz, -dy))
            def _():
                near_copies(phase, i).wait_recv()

    def near_send(phase):
        for i, (dz, dy) in enumerate(NEAR):
            @pl.when(inside(dz, dy))
            def _():
                near_copies(phase, i).wait_send()

    near_start(0)

    for i, yt in both:
        @pl.when(relays_x[i])
        def _():
            x_first(i, yt).wait_recv()
            x_second(i, yt).start()

    def blur_zy(xi, phase):
        columns = []
        layer = xi - 16 * phase
        to_low, to_high = lax.rem(128 - 8 * layer, 128), 120 - 8 * layer
        for zt in range(3):
            halo = jnp.where(lane < 64, pltpu.roll(HB[zt, 1, phase], to_low, 1), pltpu.roll(HB[zt, 0, phase], to_high, 1))
            columns.append([B[zt, 0, xi], B[zt, 1, xi], halo])
        inner, outer = [], []
        for yt in range(3):
            a, b = wide_z(columns[0][yt], columns[1][yt], columns[2][yt], row)
            inner.append(a)
            outer.append(b)
        place = lax.rem(xi + 5, 27)
        for zt, tiles in enumerate((inner, outer)):
            for yt in range(3):
                C[place, zt, yt] = taps_sum([ring_y(tiles, yt, j, lane) for j in range(-2, 3)])

    def blur_x(p):
        for zt in range(2):
            for yt in range(3):
                BL[p, zt, yt] = taps_sum([C[p + j, zt, yt] for j in range(5)])

    above = jnp.where(gz < 15, 0.5, 0.0)
    below = jnp.where(gz > 0, 0.5, 0.0)
    right = jnp.where(gy < 3, 1.0, 0.0)
    left = jnp.where(gy > 0, 1.0, 0.0)
    z_half = (jnp.full((8, 128), 0.5, F32), jnp.where(row < 4, above, below).astype(F32))
    y_one = jnp.where(lane < 64, right, left).astype(F32)
    halves = [[z_half[0], z_half[0], z_half[0] * y_one], [z_half[1], z_half[1], z_half[1] * y_one]]

    def slopes(p):
        x_in = jnp.where(jnp.logical_or(jnp.logical_and(p < 2, gx == 0), jnp.logical_and(p > 17, gx == 7)), 0.0, 1.0)
        tiles = [[BL[p + 1, zt, yt] for yt in range(3)] for zt in range(2)]
        for zt in range(2):
            for yt in range(3):
                half = halves[zt][yt] * x_in
                slope_x = (BL[p + 2, zt, yt] - BL[p, zt, yt]) * half
                SQ[0, p, zt, yt] = slope_x * slope_x
                column = [tiles[0][yt], tiles[1][yt]]
                slope_z = (ring_z(column, zt, 1, row) - ring_z(column, zt, -1, row)) * half
                SQ[1, p, zt, yt] = slope_z * slope_z
                slope_y = (ring_y(tiles[zt], yt, 1, lane) - ring_y(tiles[zt], yt, -1, lane)) * half
                SQ[2, p, zt, yt] = slope_y * slope_y

    near_recv(0)
    loop(0, 16, lambda xi: blur_zy(xi, 0), U_BLUR)
    loop(5, 17, blur_x, U_X)
    loop(5, 15, slopes, U_SLOPE)

    for i, yt in both:
        @pl.when(gets_x[i])
        def _():
            x_second(i, yt).wait_recv()

    pack(1, range(16, 27))
    near_start(1)
    near_recv(1)
    loop(16, 27, lambda xi: blur_zy(xi, 1), U_BLUR)
    loop(0, 5, blur_x, U_X)
    loop(17, 23, blur_x, U_X)
    loop(0, 5, slopes, U_SLOPE)
    loop(15, 21, slopes, U_SLOPE)

    def diffuse(tensor):
        return 1.0 / (1.0 + tensor * (1.0 / (CONTRAST * CONTRAST)))

    def tensor_x(a, p):
        return [[taps_sum([SQ[a, p + j, zt, yt] for j in range(5)]) for yt in range(3)] for zt in range(2)]

    def tensor_z(tiles, zt):
        return [taps_sum([ring_z([tiles[0][yt], tiles[1][yt]], zt, j, row) for j in range(-2, 3)]) for yt in range(3)]

    def tensor_y(tiles, yt):
        return taps_sum([ring_y(tiles, yt, j, lane) for j in range(-2, 3)])

    z_scale = jnp.where(jnp.logical_and(row == 7, gz == 15), 0.0, 0.5 * STIFFNESS).astype(F32)

    def face_z(p):
        tiles = tensor_x(1, p)
        rows = [tensor_z(tiles, zt) for zt in range(2)]
        at = p * 8 if isinstance(p, int) else pl.multiple_of(p * 8, 8)
        for yt in range(2):
            own, halo = diffuse(tensor_y(rows[0], yt)), diffuse(tensor_y(rows[1], yt))
            GZ[yt, pl.ds(at, 8), :] = (own + ring_z([own, halo], 0, 1, row)) * z_scale
    loop(0, 16, face_z, U_FACE)

    def keep_z(j, to_left, to_next, source):
        ZA[0, j], ZA[1, j], ZA[2, j] = to_left, to_next, source

    def get_gz(j):
        return jnp.stack([GZ[yt, pl.ds(j, 16, stride=8), :] for yt in range(2)])

    def get_vz(j):
        return jnp.stack([v_ref[16 * j:16 * j + 16, 128 * yt:128 * yt + 128] for yt in range(2)])

    own_z = reduce_block(8, get_gz, get_vz, keep_z)
    for i in range(5):
        for h in range(2):
            PZ[h, i] = own_z[i][:, 8 * h:8 * h + 8, :]
    cores = pltpu.make_async_remote_copy(
        src_ref=PZ.at[1 - core], dst_ref=ZPEER, send_sem=ss_k, recv_sem=rs_k,
        device_id={"gz": other_core}, device_id_type=MESH)
    cores.start()

    def face_x(p):
        tiles = tensor_z(tensor_x(0, p), 0)
        for yt in range(2):
            BL[p, 0, yt] = diffuse(tensor_y(tiles, yt))
    loop(0, 17, face_x, U_FACE)
    last_x = jnp.where(gx == 7, 0.0, 0.5 * STIFFNESS)

    def get_gx(j):
        return (BL[j, 0, 0:2] + BL[j + 1, 0, 0:2]) * (last_x if j == 15 else 0.5 * STIFFNESS)

    def keep_x(j, to_left, to_next, source):
        XA[0, j], XA[1, j], XA[2, j] = to_left, to_next, source

    own_x = reduce_block(16, get_gx, lambda j: B[1, :, j], keep_x)
    for i in range(5):
        XOWN[i] = own_x[i]
    pair = pltpu.make_async_remote_copy(
        src_ref=XOWN, dst_ref=XPEER, send_sem=ss_p, recv_sem=rs_p,
        device_id={"gx": gx + 1 - 2 * zh}, device_id_type=MESH)
    pair.start()

    y_scale = (jnp.full((8, 128), 0.5 * STIFFNESS, F32),
               jnp.where(jnp.logical_and(lane == 127, gy == 3), 0.0, 0.5 * STIFFNESS).astype(F32))

    def face_y(p):
        tiles = tensor_z(tensor_x(2, p), 0)
        values = [diffuse(tensor_y(tiles, yt)) for yt in range(3)]
        at = p * 8 if isinstance(p, int) else pl.multiple_of(p * 8, 8)
        for yt in range(2):
            GY[yt, pl.ds(at, 8), :] = (values[yt] + ring_y(values, yt, 1, lane)) * y_scale[yt]
    loop(0, 16, face_y, U_FACE)

    cores.wait_recv()
    mine = [PZ[core, i] for i in range(5)]
    peer = [ZPEER[i] for i in range(5)]
    low = core == 0
    merged_z, middle_z = merge_blocks([jnp.where(low, a, b) for a, b in zip(mine, peer)],
                                      [jnp.where(low, b, a) for a, b in zip(mine, peer)])
    for i in range(5):
        for yt in range(2):
            MS[pl.ds(2 * i + yt, 8, stride=16), :] = merged_z[i][yt]

    def to_solver(k):
        return pltpu.make_async_remote_copy(
            src_ref=MS.at[pl.ds(32 * k, 32)], dst_ref=ZR.at[pl.ds(pl.multiple_of(zc * 32, 32), 32)],
            send_sem=ss_a.at[k], recv_sem=rs_a.at[zc],
            device_id={"gz": 2 * (FIRST_SOLVER + k) + core}, device_id_type=MESH)

    def from_chip(p):
        return pltpu.make_async_remote_copy(
            src_ref=MS.at[pl.ds(0, 32)], dst_ref=ZR.at[pl.ds(32 * p, 32)],
            send_sem=ss_a.at[0], recv_sem=rs_a.at[p],
            device_id={"gz": other_core}, device_id_type=MESH)

    for k in range(SOLVERS):
        @pl.when(zc != FIRST_SOLVER + k)
        def _():
            to_solver(k).start()

        @pl.when(zc == FIRST_SOLVER + k)
        def _():
            ZR[32 * (FIRST_SOLVER + k):32 * (FIRST_SOLVER + k) + 32, :] = MS[32 * k:32 * k + 32, :]

    for yt in range(2):
        GT[128 * yt:128 * yt + 128, :] = GY[yt].T
        VT[128 * yt:128 * yt + 128, :] = B[1, yt, 0:16].reshape(128, 128).T

    def keep_y(j, to_left, to_next, source):
        YA[0, j], YA[1, j], YA[2, j] = to_left, to_next, source

    own_y = reduce_block(32, lambda j: GT[pl.ds(j, 8, stride=32), :], lambda j: VT[pl.ds(j, 8, stride=32), :], keep_y)
    for i in range(5):
        PY[i] = own_y[i]

    def y_copy(d):
        return pltpu.make_async_remote_copy(
            src_ref=PY, dst_ref=YG.at[gy], send_sem=ss_y.at[d - 1], recv_sem=rs_y.at[d - 1],
            device_id={"gy": lax.rem(gy + d, 4)}, device_id_type=MESH)

    def y_back(d):
        return pltpu.make_async_remote_copy(
            src_ref=PY, dst_ref=YG.at[lax.rem(gy + 4 - d, 4)], send_sem=ss_y.at[d - 1], recv_sem=rs_y.at[d - 1],
            device_id={"gy": lax.rem(gy + d, 4)}, device_id_type=MESH)

    for d in (1, 2, 3):
        y_copy(d).start()
    YG[gy] = PY[...]

    place = jnp.clip(zc - FIRST_SOLVER, 0, SOLVERS - 1)

    def to_chip(p):
        return pltpu.make_async_remote_copy(
            src_ref=RT.at[pl.ds(8 * p, 8)], dst_ref=RV.at[pl.ds(pl.multiple_of(place * 8, 8), 8)],
            send_sem=ss_r.at[p], recv_sem=rs_r.at[place],
            device_id={"gz": 2 * p + core}, device_id_type=MESH)

    def from_solver(k):
        return pltpu.make_async_remote_copy(
            src_ref=RT.at[pl.ds(0, 8)], dst_ref=RV.at[pl.ds(8 * k, 8)],
            send_sem=ss_r.at[0], recv_sem=rs_r.at[k],
            device_id={"gz": other_core}, device_id_type=MESH)

    @pl.when(is_solver)
    def _():
        for p in range(8):
            @pl.when(zc != p)
            def _():
                from_chip(p).wait_recv()

        def gather(i):
            return jnp.stack([ZR[pl.ds(16 * rr + 2 * i + yt, 8, stride=32), :] for rr in range(2) for yt in range(2)])
        series, gl, gr, il, ir = [gather(i) for i in range(5)]
        sigma = ladder_rings(series, gl + pltpu.roll(gr, 1, 1), il + pltpu.roll(ir, 1, 1), 8, 1)
        following = pltpu.roll(sigma, 7, 1)
        for rr in range(2):
            for yt in range(2):
                RT[pl.ds(4 * rr + yt, 8, stride=8), :] = sigma[2 * rr + yt]
                RT[pl.ds(4 * rr + 2 + yt, 8, stride=8), :] = following[2 * rr + yt]
        for p in range(8):
            @pl.when(zc != p)
            def _():
                to_chip(p).start()

            @pl.when(zc == p)
            def _():
                RV[pl.ds(pl.multiple_of(place * 8, 8), 8), :] = RT[8 * p:8 * p + 8, :]

    for d in (1, 2, 3):
        y_back(d).wait_recv()
    series, gl, gr, il, ir = [YG[:, i].reshape(32, 128) for i in range(5)]
    sigma = ladder_rings(series, gl + pltpu.roll(gr, 1, 0), il + pltpu.roll(ir, 1, 0), 32, 0)
    YS[0] = sigma.reshape(4, 8, 128)
    YS[1] = pltpu.roll(sigma, 31, 0).reshape(4, 8, 128)
    first, solved = YS[0, gy], YS[1, gy]
    VT[pl.ds(0, 8, stride=32), :] = first
    for j in range(31, 0, -1):
        solved = YA[2, j] + YA[0, j] * first + YA[1, j] * solved
        VT[pl.ds(j, 8, stride=32), :] = solved
    for yt in range(2):
        XY[yt] = VT[128 * yt:128 * yt + 128, :].T

    pair.wait_recv()
    mine = [XOWN[i] for i in range(5)]
    peer = [XPEER[i] for i in range(5)]
    low_x = zh == 0
    merged_x, middle_x = merge_blocks([jnp.where(low_x, a, b) for a, b in zip(mine, peer)],
                                      [jnp.where(low_x, b, a) for a, b in zip(mine, peer)])
    for i in range(5):
        XG[xc, i] = merged_x[i]

    def xg_copy(d):
        return pltpu.make_async_remote_copy(
            src_ref=XG.at[xc], dst_ref=XG.at[xc], send_sem=ss_c.at[d - 1], recv_sem=rs_c.at[d - 1],
            device_id={"gx": lax.rem(gx + 2 * d, 8)}, device_id_type=MESH)

    def xg_back(d):
        return pltpu.make_async_remote_copy(
            src_ref=XG.at[xc], dst_ref=XG.at[lax.rem(xc + 4 - d, 4)], send_sem=ss_c.at[d - 1], recv_sem=rs_c.at[d - 1],
            device_id={"gx": lax.rem(gx + 2 * d, 8)}, device_id_type=MESH)

    for d in (1, 2, 3):
        xg_copy(d).start()

    for k in range(SOLVERS):
        @pl.when(zc != FIRST_SOLVER + k)
        def _():
            from_solver(k).wait_recv()

    def ends(w):
        return jnp.stack([RV[pl.ds(2 * w + yt, 8, stride=4), :] for yt in range(2)])
    start, end = ends(0), ends(1)
    middle = middle_z[2] + middle_z[0] * start + middle_z[1] * end
    SEP[core, 0] = jnp.where(low, start, middle)
    SEP[core, 1] = jnp.where(low, middle, end)
    GIVE[0] = jnp.where(low, middle, start)
    GIVE[1] = jnp.where(low, end, middle)
    give = pltpu.make_async_remote_copy(
        src_ref=GIVE, dst_ref=SEP.at[core], send_sem=ss_b, recv_sem=rs_b,
        device_id={"gz": other_core}, device_id_type=MESH)
    give.start()

    for d in (1, 2, 3):
        xg_back(d).wait_recv()
    ground, source = XG[0, 1], XG[0, 3]
    stack = []
    for p in range(4):
        series = XG[p, 0]
        inverse = 1.0 / (ground + series)
        ratio = series * inverse
        stack.append((source * inverse, ratio))
        if p < 3:
            ground = XG[p + 1, 1] + XG[p, 2] + ratio * ground
            source = XG[p + 1, 3] + XG[p, 4] + ratio * source
    value = stack[3][0]
    SG[4] = jnp.zeros((2, 8, 128), F32)
    SG[3] = value
    for p in (2, 1, 0):
        value = stack[p][0] + stack[p][1] * value
        SG[p] = value
    start_x, end_x = SG[xc], SG[xc + 1]
    middle_node = middle_x[2] + middle_x[0] * start_x + middle_x[1] * end_x
    first = jnp.where(low_x, start_x, middle_node)
    solved = jnp.where(low_x, middle_node, end_x)

    def add_x(j, value):
        for yt in range(2):
            XY[yt, 8 * j:8 * j + 8, :] = XY[yt, 8 * j:8 * j + 8, :] + value[yt]
    add_x(0, first)
    for j in range(15, 0, -1):
        solved = XA[2, j] + XA[0, j] * first + XA[1, j] * solved
        add_x(j, solved)

    pltpu.make_async_remote_copy(
        src_ref=GIVE, dst_ref=SEP.at[1 - core], send_sem=ss_b, recv_sem=rs_b,
        device_id={"gz": other_core}, device_id_type=MESH).wait_recv()
    first = jnp.concatenate([SEP[0, 0], SEP[1, 0]], axis=1)
    solved = jnp.concatenate([SEP[0, 1], SEP[1, 1]], axis=1)

    def write(j, value):
        for yt in range(2):
            o_ref[16 * j:16 * j + 16, 128 * yt:128 * yt + 128] = value[yt] + XY[yt, pl.ds(j, 16, stride=8), :]
    write(0, first)
    for j in range(7, 0, -1):
        solved = ZA[2, j] + ZA[0, j] * first + ZA[1, j] * solved
        write(j, solved)

    for i, yt in both:
        @pl.when(sends_x[i])
        def _():
            x_first(i, yt).wait_send()

        @pl.when(relays_x[i])
        def _():
            x_second(i, yt).wait_send()
    near_send(0)
    near_send(1)
    pair.wait_send()
    for d in (1, 2, 3):
        y_copy(d).wait_send()
        xg_copy(d).wait_send()
    for k in range(SOLVERS):
        @pl.when(zc != FIRST_SOLVER + k)
        def _():
            to_solver(k).wait_send()

    @pl.when(is_solver)
    def _():
        for p in range(8):
            @pl.when(zc != p)
            def _():
                to_chip(p).wait_send()
    cores.wait_send()
    give.wait_send()


def body(volume):
    tile = (8, 128)
    dma = pltpu.SemaphoreType.DMA
    vmem = [
        (128, 256),
        (3, 2, 27) + tile,
        (2, 2) + tile,
        (3, 2, 2) + tile,
        (2, 6) + tile,
        (2, 5) + tile,
        (27, 2, 3) + tile,
        (23, 2, 3) + tile,
        (3, 21, 2, 3) + tile,
        (2, 128, 128),
        (2, 128, 128),
        (3, 16, 2) + tile,
        (5, 2) + tile,
        (5, 2) + tile,
        (4, 5, 2) + tile,
        (5, 2) + tile,
        (3, 8, 2, 16, 128),
        (2, 5, 2) + tile,
        (5, 2) + tile,
        (128, 128),
        (256, 128),
        (64, 128),
        (32, 128),
        (2, 2, 2) + tile,
        (256, 128),
        (256, 128),
        (3, 32) + tile,
        (5,) + tile,
        (4, 5) + tile,
        (2, 4) + tile,
        (2, 128, 128),
        (2, 2) + tile,
    ]
    sems = [None, (2, 8), (2, 8), (2, 2), (2, 2), (2, 2), (2, 2), None, None, (3,), (3,), (3,), (3,), None, None, (4,), (8,), (8,), (4,), None, None]
    total = pl.pallas_call(
        kernel,
        out_shape=jax.ShapeDtypeStruct((128, 256), F32),
        in_specs=[pl.BlockSpec(memory_space=pltpu.HBM)],
        out_specs=pl.BlockSpec(memory_space=pltpu.VMEM),
        scratch_shapes=[pltpu.VMEM(shape, F32) for shape in vmem] + [dma(s) if s else dma for s in sems],
        compiler_params=pltpu.CompilerParams(
            collective_id=0, has_side_effects=True, vmem_limit_bytes=24 * 2**20),
        cost_estimate=pl.CostEstimate(flops=40_000_000, bytes_accessed=262144, transcendentals=0),
    )(volume.reshape(128, 256))
    return (total / 3.0).reshape(8, 16, 256)


def solution(mesh):
    return jax.shard_map(
        body,
        mesh=mesh,
        in_specs=(P("gz", "gx", "gy"),),
        out_specs=P("gz", "gx", "gy"),
        check_vma=False,
    )
```

```python
import functools

import jax
import jax.numpy as jnp
from jax import lax
from jax.experimental import pallas as pl
from jax.experimental.pallas import tpu as pltpu
from jax.sharding import PartitionSpec as P

MESH = pl.DeviceIdType.MESH
F32 = jnp.float32
RAW_TAPS = (0.41111229, 0.8007374, 1.0, 0.8007374, 0.41111229)
TAPS = tuple(tap / sum(RAW_TAPS) for tap in RAW_TAPS)
STIFFNESS = 9000.0
CONTRAST = 0.1
NEAR = tuple((dz, dy) for dz in (-1, 0, 1) for dy in (-1, 0, 1) if dz or dy)
NEAR_HALO = tuple((dz, dy, yt) for yt, dy_end in ((0, -1), (1, 1)) for dz in (-1, 0, 1) for dy in (0, dy_end) if dz or dy)
SOLVERS = 2
FIRST_SOLVER = 3
ROWS = 8 // SOLVERS
MESSAGE, ANSWER = 10 * ROWS, 4 * ROWS
U_BLUR, U_X, U_SLOPE, U_FACE = 4, 4, 5, 8


def roll_z(tile, j):
    return pltpu.roll(tile, (-j) % 8, tile.ndim - 2)


def roll_y(tile, j):
    return pltpu.roll(tile, (-j) % 128, tile.ndim - 1)


def taps_sum(parts):
    return TAPS[2] * parts[2] + TAPS[1] * (parts[1] + parts[3]) + TAPS[0] * (parts[0] + parts[4])


def ring_z(tiles, t, j, row):
    if j == 0:
        return tiles[t]
    if j > 0:
        return jnp.where(row < 8 - j, roll_z(tiles[t], j), roll_z(tiles[1 - t], j))
    return jnp.where(row >= -j, roll_z(tiles[t], j), roll_z(tiles[1 - t], j))


def ring_y(tiles, t, j, lane):
    if j == 0:
        return tiles[t]
    if j > 0:
        return jnp.where(lane < 128 - j, roll_y(tiles[t], j), roll_y(tiles[(t + 1) % 3], j))
    return jnp.where(lane >= -j, roll_y(tiles[t], j), roll_y(tiles[(t + 2) % 3], j))


def wide_z(down, own, up, row):
    inner, outer = [], []
    for j in range(-2, 3):
        if j == 0:
            inner.append(own)
            outer.append(jnp.where(row < 4, up, down))
            continue
        down_j, own_j, up_j = roll_z(down, j), roll_z(own, j), roll_z(up, j)
        if j > 0:
            inner.append(jnp.where(row < 8 - j, own_j, up_j))
            outer.append(jnp.where(row < 4, up_j, jnp.where(row < 8 - j, down_j, own_j)))
        else:
            inner.append(jnp.where(row >= -j, own_j, down_j))
            outer.append(jnp.where(row >= 4, down_j, jnp.where(row >= -j, up_j, own_j)))
    return taps_sum(inner), taps_sum(outer)


def loop(first, last, step, unroll):
    trips = (last - first) // unroll

    def some(t, carry):
        for u in range(unroll):
            step(first + t * unroll + u)
        return carry
    if trips:
        lax.fori_loop(0, trips, some, 0)
    for i in range(first + trips * unroll, last):
        step(i)


def reduce_block(count, get_face, get_value, keep):
    series = get_face(0)
    left_ground = jnp.ones_like(series)
    left_source = get_value(0)
    ground = jnp.ones_like(series)
    source = get_value(1)
    for j in range(1, count):
        face = get_face(j)
        inverse = 1.0 / (series + ground + face)
        to_left, to_next = series * inverse, face * inverse
        keep(j, to_left, to_next, source * inverse)
        left_ground = left_ground + to_left * ground
        left_source = left_source + to_left * source
        series = to_left * face
        if j < count - 1:
            ground = 1.0 + to_next * ground
            source = get_value(j + 1) + to_next * source
    return series, left_ground, to_next * ground, left_source, to_next * source


def merge_blocks(left, right):
    a_l, gl_l, gr_l, il_l, ir_l = left
    a_r, gl_r, gr_r, il_r, ir_r = right
    ground, source = gr_l + gl_r, ir_l + il_r
    inverse = 1.0 / (a_l + ground + a_r)
    to_l, to_r = a_l * inverse, a_r * inverse
    merged = (to_l * a_r, gl_l + to_l * ground, gr_r + to_r * ground, il_l + to_l * source, ir_r + to_r * source)
    return merged, (to_l, to_r, source * inverse)


def ladder_rings(series, ground, source, count, axis):
    size = series.shape[axis]
    step = 1
    while step < count:
        def low(array):
            return pltpu.roll(array, step, axis)

        def high(array):
            return pltpu.roll(array, size - step, axis)

        before = low(series)
        inverse = 1.0 / (ground + series + before)
        from_low, from_high = before * low(inverse), series * high(inverse)
        ground, source, series = (
            ground + from_low * low(ground) + from_high * high(ground),
            source + from_low * low(source) + from_high * high(source),
            from_high * high(series),
        )
        step *= 2
    return source / ground


def kernel(v_hbm, o_ref, v_ref, B, HS, HB, C, BL, SQ, GZ, GY, XA, XOWN, XPEER, XG, SG, ZA, PZ, ZPEER,
           MS, ZR, RT, RV, SEP, GT, VT, YA, PY, YG, YS, XY, GIVE, in_sem, ss_h, rs_h, ss_x, rs_x, ss_p, rs_p,
           ss_c, rs_c, ss_y, rs_y, ss_k, rs_k, ss_a, rs_a, ss_r, rs_r, ss_b, rs_b):
    gx, gy, gz = lax.axis_index("gx"), lax.axis_index("gy"), lax.axis_index("gz")
    zc, core = lax.div(gz, 2), lax.rem(gz, 2)
    xc, zh = lax.div(gx, 2), lax.rem(gx, 2)
    other_core = gz + 1 - 2 * core
    load = pltpu.make_async_copy(v_hbm, v_ref, in_sem)
    load.start()

    row = lax.broadcasted_iota(jnp.int32, (8, 128), 0)
    lane = lax.broadcasted_iota(jnp.int32, (8, 128), 1)

    def inside(dz, dy):
        z, y = gz + dz, gy + dy
        return jnp.logical_and(jnp.logical_and(z >= 0, z < 16), jnp.logical_and(y >= 0, y < 4))

    barrier = pltpu.get_barrier_semaphore()
    always = []
    for d in (2, 4, 6):
        always.append({"gx": lax.rem(gx + d, 8)})
    for d in (1, 2, 3):
        always.append({"gy": lax.rem(gy + d, 4)})
    is_solver = jnp.logical_and(zc >= FIRST_SOLVER, zc < FIRST_SOLVER + SOLVERS)
    total = jnp.int32(len(always))

    @pl.when(gx > 0)
    def _():
        pl.semaphore_signal(barrier, inc=1, device_id={"gx": gx - 1}, device_id_type=MESH)

    @pl.when(gx < 7)
    def _():
        pl.semaphore_signal(barrier, inc=1, device_id={"gx": gx + 1}, device_id_type=MESH)

    total = total + jnp.where(gx > 0, 1, 0) + jnp.where(gx < 7, 1, 0)
    for target in always:
        pl.semaphore_signal(barrier, inc=1, device_id=target, device_id_type=MESH)
    for p in range(8):
        solves = FIRST_SOLVER <= p < FIRST_SOLVER + SOLVERS
        meets = zc != p if solves else is_solver
        total = total + jnp.where(meets, 1, 0)

        @pl.when(meets)
        def _():
            pl.semaphore_signal(barrier, inc=1, device_id={"gz": 2 * p + core}, device_id_type=MESH)
    for dz, dy in NEAR:
        total = total + jnp.where(inside(dz, dy), 1, 0)

        @pl.when(inside(dz, dy))
        def _():
            pl.semaphore_signal(barrier, inc=1, device_id={"gz": gz + dz, "gy": gy + dy}, device_id_type=MESH)

    def pack(phase, layers, yt):
        packed = None
        for i, x in enumerate(layers):
            shift = (8 * i + 8 * yt) % 128
            tile = pltpu.roll(B[1, yt, x], shift, 1) if shift else B[1, yt, x]
            packed = tile if packed is None else jnp.where(lane < 8 * i, packed, tile)
        HS[yt, phase] = packed

    load.wait()
    for yt in range(2):
        XY[yt] = v_ref[:, 128 * yt:128 * yt + 128]
    for x in range(16):
        for yt in range(2):
            B[1, yt, x] = XY[yt, pl.ds(x, 8, stride=16), :]
    pack(0, range(16), 0)
    pack(0, range(16), 1)

    @pl.when(gz == 0)
    def _():
        B[0] = jnp.zeros((2, 27, 8, 128), F32)
        HB[0] = jnp.zeros((2, 2, 8, 128), F32)

    @pl.when(gz == 15)
    def _():
        B[2] = jnp.zeros((2, 27, 8, 128), F32)
        HB[2] = jnp.zeros((2, 2, 8, 128), F32)

    @pl.when(gy == 0)
    def _():
        for zt in range(3):
            HB[zt, 0] = jnp.zeros((2, 8, 128), F32)

    @pl.when(gy == 3)
    def _():
        for zt in range(3):
            HB[zt, 1] = jnp.zeros((2, 8, 128), F32)

    @pl.when(gx == 0)
    def _():
        for yt in range(2):
            B[1, yt, 22:27] = jnp.zeros((5, 8, 128), F32)

    @pl.when(gx == 7)
    def _():
        for yt in range(2):
            B[1, yt, 16:22] = jnp.zeros((6, 8, 128), F32)

    pl.semaphore_wait(barrier, total)

    def x_copy(i, yt):
        source, target, device = ((B.at[1, yt, 0:6], B.at[1, yt, 16:22], {"gx": gx - 1}),
                                  (B.at[1, yt, 11:16], B.at[1, yt, 22:27], {"gx": gx + 1}))[i]
        return pltpu.make_async_remote_copy(
            src_ref=source, dst_ref=target, send_sem=ss_x.at[i, yt], recv_sem=rs_x.at[i, yt],
            device_id=device, device_id_type=MESH)

    sends_x = (gx > 0, gx < 7)
    gets_x = (gx < 7, gx > 0)
    both = [(i, yt) for yt in range(2) for i in range(2)]

    for i, yt in both:
        @pl.when(sends_x[i])
        def _():
            x_copy(i, yt).start()

    def near_copy(phase, i):
        if phase == 0:
            dz, dy = NEAR[i]
            ys, xs = slice(0, 2), slice(0, 16)
        else:
            dz, dy, yt = NEAR_HALO[i]
            ys, xs = yt, slice(16, 27)
        if dy == 0:
            source, target = B.at[1, ys, xs], B.at[1 - dz, ys, xs]
        elif dy == 1:
            source, target = HS.at[1, phase], HB.at[1 - dz, 0, phase]
        else:
            source, target = HS.at[0, phase], HB.at[1 - dz, 1, phase]
        return pltpu.make_async_remote_copy(
            src_ref=source, dst_ref=target, send_sem=ss_h.at[phase, i], recv_sem=rs_h.at[phase, i],
            device_id={"gz": gz + dz, "gy": gy + dy}, device_id_type=MESH)

    def near_list(phase):
        return [d[:2] for d in (NEAR, NEAR_HALO)[phase]]

    def near_start(phase, first, last):
        for i, (dz, dy) in enumerate(near_list(phase)):
            if first <= i < last:
                @pl.when(inside(dz, dy))
                def _():
                    near_copy(phase, i).start()

    def near_recv(phase):
        for i, (dz, dy) in enumerate(near_list(phase)):
            @pl.when(inside(-dz, -dy))
            def _():
                near_copy(phase, i).wait_recv()

    def near_send(phase):
        for i, (dz, dy) in enumerate(near_list(phase)):
            @pl.when(inside(dz, dy))
            def _():
                near_copy(phase, i).wait_send()

    near_start(0, 0, 8)

    def blur_zy(xi, phase):
        columns = []
        layer = xi - 16 * phase
        to_low, to_high = lax.rem(128 - 8 * layer, 128), 120 - 8 * layer
        for zt in range(3):
            halo = jnp.where(lane < 64, pltpu.roll(HB[zt, 1, phase], to_low, 1), pltpu.roll(HB[zt, 0, phase], to_high, 1))
            columns.append([B[zt, 0, xi], B[zt, 1, xi], halo])
        inner, outer = [], []
        for yt in range(3):
            a, b = wide_z(columns[0][yt], columns[1][yt], columns[2][yt], row)
            inner.append(a)
            outer.append(b)
        place = lax.rem(xi + 5, 27)
        for zt, tiles in enumerate((inner, outer)):
            for yt in range(3):
                C[place, zt, yt] = taps_sum([ring_y(tiles, yt, j, lane) for j in range(-2, 3)])

    def blur_x(p):
        for zt in range(2):
            for yt in range(3):
                BL[p, zt, yt] = taps_sum([C[p + j, zt, yt] for j in range(5)])

    above = jnp.where(gz < 15, 0.5, 0.0)
    below = jnp.where(gz > 0, 0.5, 0.0)
    right = jnp.where(gy < 3, 1.0, 0.0)
    left = jnp.where(gy > 0, 1.0, 0.0)
    z_half = (jnp.full((8, 128), 0.5, F32), jnp.where(row < 4, above, below).astype(F32))
    y_one = jnp.where(lane < 64, right, left).astype(F32)
    halves = [[z_half[0], z_half[0], z_half[0] * y_one], [z_half[1], z_half[1], z_half[1] * y_one]]

    def slopes(p):
        x_in = jnp.where(jnp.logical_or(jnp.logical_and(p < 2, gx == 0), jnp.logical_and(p > 17, gx == 7)), 0.0, 1.0)
        tiles = [[BL[p + 1, zt, yt] for yt in range(3)] for zt in range(2)]
        for zt in range(2):
            for yt in range(3):
                half = halves[zt][yt] * x_in
                slope_x = (BL[p + 2, zt, yt] - BL[p, zt, yt]) * half
                SQ[0, p, zt, yt] = slope_x * slope_x
                column = [tiles[0][yt], tiles[1][yt]]
                slope_z = (ring_z(column, zt, 1, row) - ring_z(column, zt, -1, row)) * half
                SQ[1, p, zt, yt] = slope_z * slope_z
                slope_y = (ring_y(tiles[zt], yt, 1, lane) - ring_y(tiles[zt], yt, -1, lane)) * half
                SQ[2, p, zt, yt] = slope_y * slope_y

    near_recv(0)
    loop(0, 16, lambda xi: blur_zy(xi, 0), U_BLUR)
    loop(5, 17, blur_x, U_X)
    loop(5, 15, slopes, U_SLOPE)

    for yt in range(2):
        for i in range(2):
            @pl.when(gets_x[i])
            def _():
                x_copy(i, yt).wait_recv()
        pack(1, range(16, 27), yt)
        near_start(1, 5 * yt, 5 * yt + 5)
    near_recv(1)
    loop(16, 27, lambda xi: blur_zy(xi, 1), U_BLUR)
    loop(0, 5, blur_x, U_X)
    loop(17, 23, blur_x, U_X)
    loop(0, 5, slopes, U_SLOPE)
    loop(15, 21, slopes, U_SLOPE)

    def diffuse(tensor):
        return 1.0 / (1.0 + tensor * (1.0 / (CONTRAST * CONTRAST)))

    def tensor_x(a, p):
        return [[taps_sum([SQ[a, p + j, zt, yt] for j in range(5)]) for yt in range(3)] for zt in range(2)]

    def tensor_z(tiles, zt):
        return [taps_sum([ring_z([tiles[0][yt], tiles[1][yt]], zt, j, row) for j in range(-2, 3)]) for yt in range(3)]

    def tensor_y(tiles, yt):
        return taps_sum([ring_y(tiles, yt, j, lane) for j in range(-2, 3)])

    z_scale = jnp.where(jnp.logical_and(row == 7, gz == 15), 0.0, 0.5 * STIFFNESS).astype(F32)

    def face_z(p):
        tiles = tensor_x(1, p)
        rows = [tensor_z(tiles, zt) for zt in range(2)]
        at = p * 8 if isinstance(p, int) else pl.multiple_of(p * 8, 8)
        for yt in range(2):
            own, halo = diffuse(tensor_y(rows[0], yt)), diffuse(tensor_y(rows[1], yt))
            GZ[yt, pl.ds(at, 8), :] = (own + ring_z([own, halo], 0, 1, row)) * z_scale
    loop(0, 16, face_z, U_FACE)

    def keep_z(j, to_left, to_next, source):
        ZA[0, j], ZA[1, j], ZA[2, j] = to_left, to_next, source

    def get_gz(j):
        return jnp.stack([GZ[yt, pl.ds(j, 16, stride=8), :] for yt in range(2)])

    def get_vz(j):
        return jnp.stack([v_ref[16 * j:16 * j + 16, 128 * yt:128 * yt + 128] for yt in range(2)])

    own_z = reduce_block(8, get_gz, get_vz, keep_z)
    for i in range(5):
        for h in range(2):
            PZ[h, i] = own_z[i][:, 8 * h:8 * h + 8, :]
    cores = pltpu.make_async_remote_copy(
        src_ref=PZ.at[1 - core], dst_ref=ZPEER, send_sem=ss_k, recv_sem=rs_k,
        device_id={"gz": other_core}, device_id_type=MESH)
    cores.start()

    def face_x(p):
        tiles = tensor_z(tensor_x(0, p), 0)
        for yt in range(2):
            BL[p, 0, yt] = diffuse(tensor_y(tiles, yt))
    loop(0, 17, face_x, U_FACE)
    last_x = jnp.where(gx == 7, 0.0, 0.5 * STIFFNESS)

    def get_gx(j):
        return (BL[j, 0, 0:2] + BL[j + 1, 0, 0:2]) * (last_x if j == 15 else 0.5 * STIFFNESS)

    def keep_x(j, to_left, to_next, source):
        XA[0, j], XA[1, j], XA[2, j] = to_left, to_next, source

    own_x = reduce_block(16, get_gx, lambda j: B[1, :, j], keep_x)
    for i in range(5):
        XOWN[i] = own_x[i]
    pair = pltpu.make_async_remote_copy(
        src_ref=XOWN, dst_ref=XPEER, send_sem=ss_p, recv_sem=rs_p,
        device_id={"gx": gx + 1 - 2 * zh}, device_id_type=MESH)
    pair.start()

    y_scale = (jnp.full((8, 128), 0.5 * STIFFNESS, F32),
               jnp.where(jnp.logical_and(lane == 127, gy == 3), 0.0, 0.5 * STIFFNESS).astype(F32))

    def face_y(p):
        tiles = tensor_z(tensor_x(2, p), 0)
        values = [diffuse(tensor_y(tiles, yt)) for yt in range(3)]
        at = p * 8 if isinstance(p, int) else pl.multiple_of(p * 8, 8)
        for yt in range(2):
            GY[yt, pl.ds(at, 8), :] = (values[yt] + ring_y(values, yt, 1, lane)) * y_scale[yt]
    loop(0, 16, face_y, U_FACE)

    cores.wait_recv()
    mine = [PZ[core, i] for i in range(5)]
    peer = [ZPEER[i] for i in range(5)]
    low = core == 0
    merged_z, middle_z = merge_blocks([jnp.where(low, a, b) for a, b in zip(mine, peer)],
                                      [jnp.where(low, b, a) for a, b in zip(mine, peer)])
    for i in range(5):
        for yt in range(2):
            MS[pl.ds(2 * i + yt, 8, stride=10), :] = merged_z[i][yt]

    def to_solver(k):
        return pltpu.make_async_remote_copy(
            src_ref=MS.at[pl.ds(MESSAGE * k, MESSAGE)],
            dst_ref=ZR.at[pl.ds(pl.multiple_of(zc * MESSAGE, 8), MESSAGE)],
            send_sem=ss_a.at[k], recv_sem=rs_a.at[zc],
            device_id={"gz": 2 * (FIRST_SOLVER + k) + core}, device_id_type=MESH)

    def from_chip(p):
        return pltpu.make_async_remote_copy(
            src_ref=MS.at[pl.ds(0, MESSAGE)], dst_ref=ZR.at[pl.ds(MESSAGE * p, MESSAGE)],
            send_sem=ss_a.at[0], recv_sem=rs_a.at[p],
            device_id={"gz": other_core}, device_id_type=MESH)

    for k in range(SOLVERS):
        @pl.when(zc != FIRST_SOLVER + k)
        def _():
            to_solver(k).start()

        @pl.when(zc == FIRST_SOLVER + k)
        def _():
            place = MESSAGE * (FIRST_SOLVER + k)
            ZR[place:place + MESSAGE, :] = MS[MESSAGE * k:MESSAGE * k + MESSAGE, :]

    for yt in range(2):
        GT[128 * yt:128 * yt + 128, :] = GY[yt].T
        VT[128 * yt:128 * yt + 128, :] = B[1, yt, 0:16].reshape(128, 128).T

    def keep_y(j, to_left, to_next, source):
        YA[0, j], YA[1, j], YA[2, j] = to_left, to_next, source

    own_y = reduce_block(32, lambda j: GT[pl.ds(j, 8, stride=32), :], lambda j: VT[pl.ds(j, 8, stride=32), :], keep_y)
    for i in range(5):
        PY[i] = own_y[i]

    def y_copy(d):
        return pltpu.make_async_remote_copy(
            src_ref=PY, dst_ref=YG.at[gy], send_sem=ss_y.at[d - 1], recv_sem=rs_y.at[d - 1],
            device_id={"gy": lax.rem(gy + d, 4)}, device_id_type=MESH)

    def y_back(d):
        return pltpu.make_async_remote_copy(
            src_ref=PY, dst_ref=YG.at[lax.rem(gy + 4 - d, 4)], send_sem=ss_y.at[d - 1], recv_sem=rs_y.at[d - 1],
            device_id={"gy": lax.rem(gy + d, 4)}, device_id_type=MESH)

    for d in (1, 2, 3):
        y_copy(d).start()
    YG[gy] = PY[...]

    place = jnp.clip(zc - FIRST_SOLVER, 0, SOLVERS - 1)

    def to_chip(p):
        return pltpu.make_async_remote_copy(
            src_ref=RT.at[pl.ds(ANSWER * p, ANSWER)],
            dst_ref=RV.at[pl.ds(pl.multiple_of(place * ANSWER, 8), ANSWER)],
            send_sem=ss_r.at[p], recv_sem=rs_r.at[place],
            device_id={"gz": 2 * p + core}, device_id_type=MESH)

    def from_solver(k):
        return pltpu.make_async_remote_copy(
            src_ref=RT.at[pl.ds(0, ANSWER)], dst_ref=RV.at[pl.ds(ANSWER * k, ANSWER)],
            send_sem=ss_r.at[0], recv_sem=rs_r.at[k],
            device_id={"gz": other_core}, device_id_type=MESH)

    @pl.when(is_solver)
    def _():
        for p in range(8):
            @pl.when(zc != p)
            def _():
                from_chip(p).wait_recv()

        def gather(i):
            return jnp.stack([ZR[pl.ds(10 * rr + 2 * i + yt, 8, stride=MESSAGE), :] for rr in range(ROWS) for yt in range(2)])
        series, gl, gr, il, ir = [gather(i) for i in range(5)]
        sigma = ladder_rings(series, gl + pltpu.roll(gr, 1, 1), il + pltpu.roll(ir, 1, 1), 8, 1)
        following = pltpu.roll(sigma, 7, 1)
        for rr in range(ROWS):
            for yt in range(2):
                RT[pl.ds(4 * rr + yt, 8, stride=ANSWER), :] = sigma[2 * rr + yt]
                RT[pl.ds(4 * rr + 2 + yt, 8, stride=ANSWER), :] = following[2 * rr + yt]
        for p in range(8):
            @pl.when(zc != p)
            def _():
                to_chip(p).start()

            @pl.when(zc == p)
            def _():
                RV[pl.ds(pl.multiple_of(place * ANSWER, 8), ANSWER), :] = RT[ANSWER * p:ANSWER * p + ANSWER, :]

    for d in (1, 2, 3):
        y_back(d).wait_recv()
    series, gl, gr, il, ir = [YG[:, i].reshape(32, 128) for i in range(5)]
    sigma = ladder_rings(series, gl + pltpu.roll(gr, 1, 0), il + pltpu.roll(ir, 1, 0), 32, 0)
    YS[0] = sigma.reshape(4, 8, 128)
    YS[1] = pltpu.roll(sigma, 31, 0).reshape(4, 8, 128)
    first, solved = YS[0, gy], YS[1, gy]
    VT[pl.ds(0, 8, stride=32), :] = first
    for j in range(31, 0, -1):
        solved = YA[2, j] + YA[0, j] * first + YA[1, j] * solved
        VT[pl.ds(j, 8, stride=32), :] = solved
    for yt in range(2):
        XY[yt] = VT[128 * yt:128 * yt + 128, :].T

    pair.wait_recv()
    mine = [XOWN[i] for i in range(5)]
    peer = [XPEER[i] for i in range(5)]
    low_x = zh == 0
    merged_x, middle_x = merge_blocks([jnp.where(low_x, a, b) for a, b in zip(mine, peer)],
                                      [jnp.where(low_x, b, a) for a, b in zip(mine, peer)])
    for i in range(5):
        XG[xc, i] = merged_x[i]

    def xg_copy(d):
        return pltpu.make_async_remote_copy(
            src_ref=XG.at[xc], dst_ref=XG.at[xc], send_sem=ss_c.at[d - 1], recv_sem=rs_c.at[d - 1],
            device_id={"gx": lax.rem(gx + 2 * d, 8)}, device_id_type=MESH)

    def xg_back(d):
        return pltpu.make_async_remote_copy(
            src_ref=XG.at[xc], dst_ref=XG.at[lax.rem(xc + 4 - d, 4)], send_sem=ss_c.at[d - 1], recv_sem=rs_c.at[d - 1],
            device_id={"gx": lax.rem(gx + 2 * d, 8)}, device_id_type=MESH)

    for d in (1, 2, 3):
        xg_copy(d).start()

    for k in range(SOLVERS):
        @pl.when(zc != FIRST_SOLVER + k)
        def _():
            from_solver(k).wait_recv()

    def ends(w):
        return jnp.stack([RV[pl.ds(2 * w + yt, 8, stride=4), :] for yt in range(2)])
    start, end = ends(0), ends(1)
    middle = middle_z[2] + middle_z[0] * start + middle_z[1] * end
    SEP[core, 0] = jnp.where(low, start, middle)
    SEP[core, 1] = jnp.where(low, middle, end)
    GIVE[0] = jnp.where(low, middle, start)
    GIVE[1] = jnp.where(low, end, middle)
    give = pltpu.make_async_remote_copy(
        src_ref=GIVE, dst_ref=SEP.at[core], send_sem=ss_b, recv_sem=rs_b,
        device_id={"gz": other_core}, device_id_type=MESH)
    give.start()

    for d in (1, 2, 3):
        xg_back(d).wait_recv()
    ground, source = XG[0, 1], XG[0, 3]
    stack = []
    for p in range(4):
        series = XG[p, 0]
        inverse = 1.0 / (ground + series)
        ratio = series * inverse
        stack.append((source * inverse, ratio))
        if p < 3:
            ground = XG[p + 1, 1] + XG[p, 2] + ratio * ground
            source = XG[p + 1, 3] + XG[p, 4] + ratio * source
    value = stack[3][0]
    SG[4] = jnp.zeros((2, 8, 128), F32)
    SG[3] = value
    for p in (2, 1, 0):
        value = stack[p][0] + stack[p][1] * value
        SG[p] = value
    start_x, end_x = SG[xc], SG[xc + 1]
    middle_node = middle_x[2] + middle_x[0] * start_x + middle_x[1] * end_x
    first = jnp.where(low_x, start_x, middle_node)
    solved = jnp.where(low_x, middle_node, end_x)

    def add_x(j, value):
        for yt in range(2):
            XY[yt, 8 * j:8 * j + 8, :] = XY[yt, 8 * j:8 * j + 8, :] + value[yt]
    add_x(0, first)
    for j in range(15, 0, -1):
        solved = XA[2, j] + XA[0, j] * first + XA[1, j] * solved
        add_x(j, solved)

    pltpu.make_async_remote_copy(
        src_ref=GIVE, dst_ref=SEP.at[1 - core], send_sem=ss_b, recv_sem=rs_b,
        device_id={"gz": other_core}, device_id_type=MESH).wait_recv()
    first = jnp.concatenate([SEP[0, 0], SEP[1, 0]], axis=1)
    solved = jnp.concatenate([SEP[0, 1], SEP[1, 1]], axis=1)

    def write(j, value):
        for yt in range(2):
            o_ref[16 * j:16 * j + 16, 128 * yt:128 * yt + 128] = value[yt] + XY[yt, pl.ds(j, 16, stride=8), :]
    write(0, first)
    for j in range(7, 0, -1):
        solved = ZA[2, j] + ZA[0, j] * first + ZA[1, j] * solved
        write(j, solved)

    for i, yt in both:
        @pl.when(sends_x[i])
        def _():
            x_copy(i, yt).wait_send()
    near_send(0)
    near_send(1)
    pair.wait_send()
    for d in (1, 2, 3):
        y_copy(d).wait_send()
        xg_copy(d).wait_send()
    for k in range(SOLVERS):
        @pl.when(zc != FIRST_SOLVER + k)
        def _():
            to_solver(k).wait_send()

    @pl.when(is_solver)
    def _():
        for p in range(8):
            @pl.when(zc != p)
            def _():
                to_chip(p).wait_send()
    cores.wait_send()
    give.wait_send()


def body(volume):
    tile = (8, 128)
    dma = pltpu.SemaphoreType.DMA
    vmem = [
        (128, 256),
        (3, 2, 27) + tile,
        (2, 2) + tile,
        (3, 2, 2) + tile,
        (27, 2, 3) + tile,
        (23, 2, 3) + tile,
        (3, 21, 2, 3) + tile,
        (2, 128, 128),
        (2, 128, 128),
        (3, 16, 2) + tile,
        (5, 2) + tile,
        (5, 2) + tile,
        (4, 5, 2) + tile,
        (5, 2) + tile,
        (3, 8, 2, 16, 128),
        (2, 5, 2) + tile,
        (5, 2) + tile,
        (80, 128),
        (8 * MESSAGE, 128),
        (8 * ANSWER, 128),
        (32, 128),
        (2, 2, 2) + tile,
        (256, 128),
        (256, 128),
        (3, 32) + tile,
        (5,) + tile,
        (4, 5) + tile,
        (2, 4) + tile,
        (2, 128, 128),
        (2, 2) + tile,
    ]
    sems = [None, (2, 10), (2, 10), (2, 2), (2, 2), None, None, (3,), (3,), (3,), (3,), None, None, (4,), (8,), (8,), (4,), None, None]
    total = pl.pallas_call(
        kernel,
        out_shape=jax.ShapeDtypeStruct((128, 256), F32),
        in_specs=[pl.BlockSpec(memory_space=pltpu.HBM)],
        out_specs=pl.BlockSpec(memory_space=pltpu.VMEM),
        scratch_shapes=[pltpu.VMEM(shape, F32) for shape in vmem] + [dma(s) if s else dma for s in sems],
        compiler_params=pltpu.CompilerParams(
            collective_id=0, has_side_effects=True, vmem_limit_bytes=24 * 2**20),
        cost_estimate=pl.CostEstimate(flops=40_000_000, bytes_accessed=262144, transcendentals=0),
    )(volume.reshape(128, 256))
    return (total / 3.0).reshape(8, 16, 256)


def solution(mesh):
    return jax.shard_map(
        body,
        mesh=mesh,
        in_specs=(P("gz", "gx", "gy"),),
        out_specs=P("gz", "gx", "gy"),
        check_vma=False,
    )
```

```python
import functools

import jax
import jax.numpy as jnp
from jax import lax
from jax.experimental import pallas as pl
from jax.experimental.pallas import tpu as pltpu
from jax.sharding import PartitionSpec as P

MESH = pl.DeviceIdType.MESH
F32 = jnp.float32
RAW_TAPS = (0.41111229, 0.8007374, 1.0, 0.8007374, 0.41111229)
TAPS = tuple(tap / sum(RAW_TAPS) for tap in RAW_TAPS)
STIFFNESS = 9000.0
CONTRAST = 0.1
NEAR = tuple((dz, dy) for dz in (-1, 0, 1) for dy in (-1, 0, 1) if dz or dy)
NEAR_HALO = tuple((dz, dy, yt) for yt, dy_end in ((0, -1), (1, 1)) for dz in (-1, 0, 1) for dy in (0, dy_end) if dz or dy)
SOLVERS = 2
FIRST_SOLVER = 3
ROWS = 8 // SOLVERS
MESSAGE, ANSWER = 10 * ROWS, 4 * ROWS
U_BLUR, U_X, U_SLOPE, U_FACE = 4, 4, 5, 8


def roll_z(tile, j):
    return pltpu.roll(tile, (-j) % 8, tile.ndim - 2)


def roll_y(tile, j):
    return pltpu.roll(tile, (-j) % 128, tile.ndim - 1)


def taps_sum(parts):
    return TAPS[2] * parts[2] + TAPS[1] * (parts[1] + parts[3]) + TAPS[0] * (parts[0] + parts[4])


def ring_z(tiles, t, j, row):
    if j == 0:
        return tiles[t]
    if j > 0:
        return jnp.where(row < 8 - j, roll_z(tiles[t], j), roll_z(tiles[1 - t], j))
    return jnp.where(row >= -j, roll_z(tiles[t], j), roll_z(tiles[1 - t], j))


def ring_y(tiles, t, j, lane):
    if j == 0:
        return tiles[t]
    if j > 0:
        return jnp.where(lane < 128 - j, roll_y(tiles[t], j), roll_y(tiles[(t + 1) % 3], j))
    return jnp.where(lane >= -j, roll_y(tiles[t], j), roll_y(tiles[(t + 2) % 3], j))


def wide_z(down, own, up, row):
    inner, outer = [], []
    for j in range(-2, 3):
        if j == 0:
            inner.append(own)
            outer.append(jnp.where(row < 4, up, down))
            continue
        down_j, own_j, up_j = roll_z(down, j), roll_z(own, j), roll_z(up, j)
        if j > 0:
            inner.append(jnp.where(row < 8 - j, own_j, up_j))
            outer.append(jnp.where(row < 4, up_j, jnp.where(row < 8 - j, down_j, own_j)))
        else:
            inner.append(jnp.where(row >= -j, own_j, down_j))
            outer.append(jnp.where(row >= 4, down_j, jnp.where(row >= -j, up_j, own_j)))
    return taps_sum(inner), taps_sum(outer)


def loop(first, last, step, unroll):
    trips = (last - first) // unroll

    def some(t, carry):
        for u in range(unroll):
            step(first + t * unroll + u)
        return carry
    if trips:
        lax.fori_loop(0, trips, some, 0)
    for i in range(first + trips * unroll, last):
        step(i)


def reduce_block(count, get_face, get_value, keep):
    series = get_face(0)
    left_ground = jnp.ones_like(series)
    left_source = get_value(0)
    ground = jnp.ones_like(series)
    source = get_value(1)
    for j in range(1, count):
        face = get_face(j)
        inverse = 1.0 / (series + ground + face)
        to_left, to_next = series * inverse, face * inverse
        keep(j, to_left, to_next, source * inverse)
        left_ground = left_ground + to_left * ground
        left_source = left_source + to_left * source
        series = to_left * face
        if j < count - 1:
            ground = 1.0 + to_next * ground
            source = get_value(j + 1) + to_next * source
    return series, left_ground, to_next * ground, left_source, to_next * source


def merge_blocks(left, right):
    a_l, gl_l, gr_l, il_l, ir_l = left
    a_r, gl_r, gr_r, il_r, ir_r = right
    ground, source = gr_l + gl_r, ir_l + il_r
    inverse = 1.0 / (a_l + ground + a_r)
    to_l, to_r = a_l * inverse, a_r * inverse
    merged = (to_l * a_r, gl_l + to_l * ground, gr_r + to_r * ground, il_l + to_l * source, ir_r + to_r * source)
    return merged, (to_l, to_r, source * inverse)


def ladder_rings(series, ground, source, count, axis):
    size = series.shape[axis]
    step = 1
    while step < count:
        def low(array):
            return pltpu.roll(array, step, axis)

        def high(array):
            return pltpu.roll(array, size - step, axis)

        before = low(series)
        inverse = 1.0 / (ground + series + before)
        from_low, from_high = before * low(inverse), series * high(inverse)
        ground, source, series = (
            ground + from_low * low(ground) + from_high * high(ground),
            source + from_low * low(source) + from_high * high(source),
            from_high * high(series),
        )
        step *= 2
    return source / ground


def kernel(v_hbm, o_ref, v_ref, B, HS, HB, C, BL, SQ, GX, GZ, GY, XA, XOWN, XPEER, XG, SG, ZA, PZ, ZPEER,
           MS, ZR, RT, RV, GT, VT, YA, PY, YG, YS, XY, in_sem, ss_h, rs_h, ss_x, rs_x, ss_p, rs_p,
           ss_c, rs_c, ss_y, rs_y, ss_k, rs_k, ss_a, rs_a, ss_r, rs_r):
    gx, gy, gz = lax.axis_index("gx"), lax.axis_index("gy"), lax.axis_index("gz")
    zc, core = lax.div(gz, 2), lax.rem(gz, 2)
    xc, zh = lax.div(gx, 2), lax.rem(gx, 2)
    other_core = gz + 1 - 2 * core
    load = pltpu.make_async_copy(v_hbm, v_ref, in_sem)
    load.start()

    row = lax.broadcasted_iota(jnp.int32, (8, 128), 0)
    lane = lax.broadcasted_iota(jnp.int32, (8, 128), 1)

    def inside(dz, dy):
        z, y = gz + dz, gy + dy
        return jnp.logical_and(jnp.logical_and(z >= 0, z < 16), jnp.logical_and(y >= 0, y < 4))

    barrier = pltpu.get_barrier_semaphore()
    always = []
    for d in (2, 4, 6):
        always.append({"gx": lax.rem(gx + d, 8)})
    for d in (1, 2, 3):
        always.append({"gy": lax.rem(gy + d, 4)})
    is_solver = jnp.logical_and(zc >= FIRST_SOLVER, zc < FIRST_SOLVER + SOLVERS)
    total = jnp.int32(len(always))

    @pl.when(gx > 0)
    def _():
        pl.semaphore_signal(barrier, inc=1, device_id={"gx": gx - 1}, device_id_type=MESH)

    @pl.when(gx < 7)
    def _():
        pl.semaphore_signal(barrier, inc=1, device_id={"gx": gx + 1}, device_id_type=MESH)

    total = total + jnp.where(gx > 0, 1, 0) + jnp.where(gx < 7, 1, 0)
    for target in always:
        pl.semaphore_signal(barrier, inc=1, device_id=target, device_id_type=MESH)
    for p in range(8):
        solves = FIRST_SOLVER <= p < FIRST_SOLVER + SOLVERS
        meets = zc != p if solves else is_solver
        total = total + jnp.where(meets, 1, 0)

        @pl.when(meets)
        def _():
            pl.semaphore_signal(barrier, inc=1, device_id={"gz": 2 * p + core}, device_id_type=MESH)
    for dz, dy in NEAR:
        total = total + jnp.where(inside(dz, dy), 1, 0)

        @pl.when(inside(dz, dy))
        def _():
            pl.semaphore_signal(barrier, inc=1, device_id={"gz": gz + dz, "gy": gy + dy}, device_id_type=MESH)

    def pack(phase, layers, yt):
        packed = None
        for i, x in enumerate(layers):
            shift = (8 * i + 8 * yt) % 128
            tile = pltpu.roll(B[1, yt, x], shift, 1) if shift else B[1, yt, x]
            packed = tile if packed is None else jnp.where(lane < 8 * i, packed, tile)
        HS[yt, phase] = packed

    load.wait()
    for yt in range(2):
        XY[yt] = v_ref[:, 128 * yt:128 * yt + 128]
    for x in range(16):
        for yt in range(2):
            B[1, yt, x] = XY[yt, pl.ds(x, 8, stride=16), :]
    pack(0, range(16), 0)
    pack(0, range(16), 1)

    @pl.when(gz == 0)
    def _():
        B[0] = jnp.zeros((2, 27, 8, 128), F32)
        HB[0] = jnp.zeros((2, 2, 8, 128), F32)

    @pl.when(gz == 15)
    def _():
        B[2] = jnp.zeros((2, 27, 8, 128), F32)
        HB[2] = jnp.zeros((2, 2, 8, 128), F32)

    @pl.when(gy == 0)
    def _():
        for zt in range(3):
            HB[zt, 0] = jnp.zeros((2, 8, 128), F32)

    @pl.when(gy == 3)
    def _():
        for zt in range(3):
            HB[zt, 1] = jnp.zeros((2, 8, 128), F32)

    @pl.when(gx == 0)
    def _():
        for yt in range(2):
            B[1, yt, 22:27] = jnp.zeros((5, 8, 128), F32)

    @pl.when(gx == 7)
    def _():
        for yt in range(2):
            B[1, yt, 16:22] = jnp.zeros((6, 8, 128), F32)

    pl.semaphore_wait(barrier, total)

    def x_copy(i, yt):
        source, target, device = ((B.at[1, yt, 0:6], B.at[1, yt, 16:22], {"gx": gx - 1}),
                                  (B.at[1, yt, 11:16], B.at[1, yt, 22:27], {"gx": gx + 1}))[i]
        return pltpu.make_async_remote_copy(
            src_ref=source, dst_ref=target, send_sem=ss_x.at[i, yt], recv_sem=rs_x.at[i, yt],
            device_id=device, device_id_type=MESH)

    sends_x = (gx > 0, gx < 7)
    gets_x = (gx < 7, gx > 0)
    both = [(i, yt) for yt in range(2) for i in range(2)]

    for i, yt in both:
        @pl.when(sends_x[i])
        def _():
            x_copy(i, yt).start()

    def near_copy(phase, i):
        if phase == 0:
            dz, dy = NEAR[i]
            ys, xs = slice(0, 2), slice(0, 16)
        else:
            dz, dy, yt = NEAR_HALO[i]
            ys, xs = yt, slice(16, 27)
        if dy == 0:
            source, target = B.at[1, ys, xs], B.at[1 - dz, ys, xs]
        elif dy == 1:
            source, target = HS.at[1, phase], HB.at[1 - dz, 0, phase]
        else:
            source, target = HS.at[0, phase], HB.at[1 - dz, 1, phase]
        return pltpu.make_async_remote_copy(
            src_ref=source, dst_ref=target, send_sem=ss_h.at[phase, i], recv_sem=rs_h.at[phase, i],
            device_id={"gz": gz + dz, "gy": gy + dy}, device_id_type=MESH)

    def near_list(phase):
        return [d[:2] for d in (NEAR, NEAR_HALO)[phase]]

    def near_start(phase, first, last):
        for i, (dz, dy) in enumerate(near_list(phase)):
            if first <= i < last:
                @pl.when(inside(dz, dy))
                def _():
                    near_copy(phase, i).start()

    def near_recv(phase):
        for i, (dz, dy) in enumerate(near_list(phase)):
            @pl.when(inside(-dz, -dy))
            def _():
                near_copy(phase, i).wait_recv()

    def near_send(phase):
        for i, (dz, dy) in enumerate(near_list(phase)):
            @pl.when(inside(dz, dy))
            def _():
                near_copy(phase, i).wait_send()

    near_start(0, 0, 8)

    def blur_zy(xi, phase):
        columns = []
        layer = xi - 16 * phase
        to_low, to_high = lax.rem(128 - 8 * layer, 128), 120 - 8 * layer
        for zt in range(3):
            halo = jnp.where(lane < 64, pltpu.roll(HB[zt, 1, phase], to_low, 1), pltpu.roll(HB[zt, 0, phase], to_high, 1))
            columns.append([B[zt, 0, xi], B[zt, 1, xi], halo])
        inner, outer = [], []
        for yt in range(3):
            a, b = wide_z(columns[0][yt], columns[1][yt], columns[2][yt], row)
            inner.append(a)
            outer.append(b)
        place = lax.rem(xi + 5, 27)
        for zt, tiles in enumerate((inner, outer)):
            for yt in range(3):
                C[place, zt, yt] = taps_sum([ring_y(tiles, yt, j, lane) for j in range(-2, 3)])

    def blur_x(p):
        for zt in range(2):
            for yt in range(3):
                BL[p, zt, yt] = taps_sum([C[p + j, zt, yt] for j in range(5)])

    above = jnp.where(gz < 15, 0.5, 0.0)
    below = jnp.where(gz > 0, 0.5, 0.0)
    right = jnp.where(gy < 3, 1.0, 0.0)
    left = jnp.where(gy > 0, 1.0, 0.0)
    z_half = (jnp.full((8, 128), 0.5, F32), jnp.where(row < 4, above, below).astype(F32))
    y_one = jnp.where(lane < 64, right, left).astype(F32)
    halves = [[z_half[0], z_half[0], z_half[0] * y_one], [z_half[1], z_half[1], z_half[1] * y_one]]

    def slopes(p, axes):
        x_in = jnp.where(jnp.logical_or(jnp.logical_and(p < 2, gx == 0), jnp.logical_and(p > 17, gx == 7)), 0.0, 1.0)
        tiles = [[BL[p + 1, zt, yt] for yt in range(3)] for zt in range(2)]
        for zt in range(2):
            for yt in range(3):
                half = halves[zt][yt] * x_in
                for axis in axes:
                    if axis == 0:
                        change = BL[p + 2, zt, yt] - BL[p, zt, yt]
                    elif axis == 1:
                        column = [tiles[0][yt], tiles[1][yt]]
                        change = ring_z(column, zt, 1, row) - ring_z(column, zt, -1, row)
                    else:
                        change = ring_y(tiles[zt], yt, 1, lane) - ring_y(tiles[zt], yt, -1, lane)
                    slope = change * half
                    SQ[axis, p, zt, yt] = slope * slope

    def outer_slopes(axis):
        loop(0, 5, lambda p: slopes(p, (axis,)), 5)
        loop(15, 21, lambda p: slopes(p, (axis,)), 6)

    near_recv(0)
    loop(0, 16, lambda xi: blur_zy(xi, 0), U_BLUR)
    loop(5, 17, blur_x, U_X)
    loop(5, 15, lambda p: slopes(p, (0, 1, 2)), U_SLOPE)

    for yt in range(2):
        for i in range(2):
            @pl.when(gets_x[i])
            def _():
                x_copy(i, yt).wait_recv()
        pack(1, range(16, 27), yt)
        near_start(1, 5 * yt, 5 * yt + 5)
    near_recv(1)
    loop(16, 27, lambda xi: blur_zy(xi, 1), U_BLUR)
    loop(0, 5, blur_x, U_X)
    loop(17, 23, blur_x, U_X)
    outer_slopes(0)

    def diffuse(tensor):
        return 1.0 / (1.0 + tensor * (1.0 / (CONTRAST * CONTRAST)))

    def tensor_x(a, p):
        return [[taps_sum([SQ[a, p + j, zt, yt] for j in range(5)]) for yt in range(3)] for zt in range(2)]

    def tensor_z(tiles, zt):
        return [taps_sum([ring_z([tiles[0][yt], tiles[1][yt]], zt, j, row) for j in range(-2, 3)]) for yt in range(3)]

    def tensor_y(tiles, yt):
        return taps_sum([ring_y(tiles, yt, j, lane) for j in range(-2, 3)])

    def face_x(p):
        tiles = tensor_z(tensor_x(0, p), 0)
        for yt in range(2):
            GX[p, yt] = diffuse(tensor_y(tiles, yt))
    loop(0, 17, face_x, U_FACE)
    last_x = jnp.where(gx == 7, 0.0, 0.5 * STIFFNESS)

    def get_gx(j):
        return (GX[j] + GX[j + 1]) * (last_x if j == 15 else 0.5 * STIFFNESS)

    def keep_x(j, to_left, to_next, source):
        XA[0, j], XA[1, j], XA[2, j] = to_left, to_next, source

    def halves_of(get):
        return lambda j: jnp.stack([get(j), get(j + 8)])

    halved = reduce_block(8, halves_of(get_gx), halves_of(lambda j: B[1, :, j]), keep_x)
    own_x, middle_own = merge_blocks([part[0] for part in halved], [part[1] for part in halved])
    for i in range(5):
        for yt in range(2):
            XOWN[yt, i] = own_x[i][yt]

    def pair(yt):
        return pltpu.make_async_remote_copy(
            src_ref=XOWN.at[yt], dst_ref=XPEER.at[yt], send_sem=ss_p.at[yt], recv_sem=rs_p.at[yt],
            device_id={"gx": gx + 1 - 2 * zh}, device_id_type=MESH)

    for yt in range(2):
        pair(yt).start()

    z_scale = jnp.where(jnp.logical_and(row == 7, gz == 15), 0.0, 0.5 * STIFFNESS).astype(F32)

    def face_z(p):
        tiles = tensor_x(1, p)
        rows = [tensor_z(tiles, zt) for zt in range(2)]
        at = p * 8 if isinstance(p, int) else pl.multiple_of(p * 8, 8)
        for yt in range(2):
            own, halo = diffuse(tensor_y(rows[0], yt)), diffuse(tensor_y(rows[1], yt))
            GZ[yt, pl.ds(at, 8), :] = (own + ring_z([own, halo], 0, 1, row)) * z_scale
    outer_slopes(1)
    loop(0, 16, face_z, U_FACE)

    def keep_z(j, to_left, to_next, source):
        ZA[0, j], ZA[1, j], ZA[2, j] = to_left, to_next, source

    def get_gz(j):
        return jnp.stack([GZ[yt, pl.ds(j, 16, stride=8), :] for yt in range(2)])

    def get_vz(j):
        return jnp.stack([v_ref[16 * j:16 * j + 16, 128 * yt:128 * yt + 128] for yt in range(2)])

    own_z = reduce_block(8, get_gz, get_vz, keep_z)
    for i in range(5):
        for h in range(2):
            PZ[h, i] = own_z[i][:, 8 * h:8 * h + 8, :]
    cores = pltpu.make_async_remote_copy(
        src_ref=PZ, dst_ref=ZPEER, send_sem=ss_k, recv_sem=rs_k,
        device_id={"gz": other_core}, device_id_type=MESH)
    cores.start()

    y_scale = (jnp.full((8, 128), 0.5 * STIFFNESS, F32),
               jnp.where(jnp.logical_and(lane == 127, gy == 3), 0.0, 0.5 * STIFFNESS).astype(F32))

    def face_y(p):
        tiles = tensor_z(tensor_x(2, p), 0)
        values = [diffuse(tensor_y(tiles, yt)) for yt in range(3)]
        at = p * 8 if isinstance(p, int) else pl.multiple_of(p * 8, 8)
        for yt in range(2):
            GY[yt, pl.ds(at, 8), :] = (values[yt] + ring_y(values, yt, 1, lane)) * y_scale[yt]
    outer_slopes(2)
    loop(0, 16, face_y, U_FACE)

    cores.wait_recv()
    low = core == 0

    def merge_cores(half):
        mine = [PZ[half, i] for i in range(5)]
        peer = [ZPEER[half, i] for i in range(5)]
        return merge_blocks([jnp.where(low, a, b) for a, b in zip(mine, peer)],
                            [jnp.where(low, b, a) for a, b in zip(mine, peer)])

    merged_z = merge_cores(core)[0]
    for i in range(5):
        for yt in range(2):
            MS[pl.ds(2 * i + yt, 8, stride=10), :] = merged_z[i][yt]

    def to_solver(k):
        return pltpu.make_async_remote_copy(
            src_ref=MS.at[pl.ds(MESSAGE * k, MESSAGE)],
            dst_ref=ZR.at[pl.ds(pl.multiple_of(zc * MESSAGE, 8), MESSAGE)],
            send_sem=ss_a.at[k], recv_sem=rs_a.at[zc],
            device_id={"gz": 2 * (FIRST_SOLVER + k) + core}, device_id_type=MESH)

    def from_chip(p):
        return pltpu.make_async_remote_copy(
            src_ref=MS.at[pl.ds(0, MESSAGE)], dst_ref=ZR.at[pl.ds(MESSAGE * p, MESSAGE)],
            send_sem=ss_a.at[0], recv_sem=rs_a.at[p],
            device_id={"gz": other_core}, device_id_type=MESH)

    for k in range(SOLVERS):
        @pl.when(zc != FIRST_SOLVER + k)
        def _():
            to_solver(k).start()

        @pl.when(zc == FIRST_SOLVER + k)
        def _():
            place = MESSAGE * (FIRST_SOLVER + k)
            ZR[place:place + MESSAGE, :] = MS[MESSAGE * k:MESSAGE * k + MESSAGE, :]

    for yt in range(2):
        GT[128 * yt:128 * yt + 128, :] = GY[yt].T
        VT[128 * yt:128 * yt + 128, :] = B[1, yt, 0:16].reshape(128, 128).T

    def keep_y(j, to_left, to_next, source):
        YA[0, j], YA[1, j], YA[2, j] = to_left, to_next, source

    own_y = reduce_block(32, lambda j: GT[pl.ds(j, 8, stride=32), :], lambda j: VT[pl.ds(j, 8, stride=32), :], keep_y)
    for i in range(5):
        PY[i] = own_y[i]

    def y_copy(d):
        return pltpu.make_async_remote_copy(
            src_ref=PY, dst_ref=YG.at[gy], send_sem=ss_y.at[d - 1], recv_sem=rs_y.at[d - 1],
            device_id={"gy": lax.rem(gy + d, 4)}, device_id_type=MESH)

    def y_back(d):
        return pltpu.make_async_remote_copy(
            src_ref=PY, dst_ref=YG.at[lax.rem(gy + 4 - d, 4)], send_sem=ss_y.at[d - 1], recv_sem=rs_y.at[d - 1],
            device_id={"gy": lax.rem(gy + d, 4)}, device_id_type=MESH)

    for d in (1, 2, 3):
        y_copy(d).start()
    YG[gy] = PY[...]

    place = jnp.clip(zc - FIRST_SOLVER, 0, SOLVERS - 1)

    def to_chip(p, side):
        return pltpu.make_async_remote_copy(
            src_ref=RT.at[pl.ds(ANSWER * p, ANSWER)],
            dst_ref=RV.at[pl.ds(pl.multiple_of((core * SOLVERS + place) * ANSWER, 8), ANSWER)],
            send_sem=ss_r.at[side, p], recv_sem=rs_r.at[core * SOLVERS + place],
            device_id={"gz": 2 * p + (1 - core if side else core)}, device_id_type=MESH)

    def from_solver(half, k):
        at = half * SOLVERS + k
        return pltpu.make_async_remote_copy(
            src_ref=RT.at[pl.ds(0, ANSWER)], dst_ref=RV.at[pl.ds(ANSWER * at, ANSWER)],
            send_sem=ss_r.at[0, 0], recv_sem=rs_r.at[at],
            device_id={"gz": other_core}, device_id_type=MESH)

    far_first = sorted(range(8), key=lambda p: -abs(2 * p - 7))

    @pl.when(is_solver)
    def _():
        for p in range(8):
            @pl.when(zc != p)
            def _():
                from_chip(p).wait_recv()

        def gather(i):
            return jnp.stack([ZR[pl.ds(10 * rr + 2 * i + yt, 8, stride=MESSAGE), :] for rr in range(ROWS) for yt in range(2)])
        series, gl, gr, il, ir = [gather(i) for i in range(5)]
        sigma = ladder_rings(series, gl + pltpu.roll(gr, 1, 1), il + pltpu.roll(ir, 1, 1), 8, 1)
        following = pltpu.roll(sigma, 7, 1)
        for rr in range(ROWS):
            for yt in range(2):
                RT[pl.ds(4 * rr + yt, 8, stride=ANSWER), :] = sigma[2 * rr + yt]
                RT[pl.ds(4 * rr + 2 + yt, 8, stride=ANSWER), :] = following[2 * rr + yt]
        for p in far_first:
            to_chip(p, 1).start()

            @pl.when(zc != p)
            def _():
                to_chip(p, 0).start()

            @pl.when(zc == p)
            def _():
                at = pl.multiple_of((core * SOLVERS + place) * ANSWER, 8)
                RV[pl.ds(at, ANSWER), :] = RT[ANSWER * p:ANSWER * p + ANSWER, :]

    for d in (1, 2, 3):
        y_back(d).wait_recv()
    series, gl, gr, il, ir = [YG[:, i].reshape(32, 128) for i in range(5)]
    sigma = ladder_rings(series, gl + pltpu.roll(gr, 1, 0), il + pltpu.roll(ir, 1, 0), 32, 0)
    YS[0] = sigma.reshape(4, 8, 128)
    YS[1] = pltpu.roll(sigma, 31, 0).reshape(4, 8, 128)
    first, solved = YS[0, gy], YS[1, gy]
    VT[pl.ds(0, 8, stride=32), :] = first
    for j in range(31, 0, -1):
        solved = YA[2, j] + YA[0, j] * first + YA[1, j] * solved
        VT[pl.ds(j, 8, stride=32), :] = solved
    for yt in range(2):
        XY[yt] = VT[128 * yt:128 * yt + 128, :].T

    low_x = zh == 0

    def xg_copy(yt, d):
        return pltpu.make_async_remote_copy(
            src_ref=XG.at[xc, yt], dst_ref=XG.at[xc, yt], send_sem=ss_c.at[yt, d - 1], recv_sem=rs_c.at[yt, d - 1],
            device_id={"gx": lax.rem(gx + 2 * d, 8)}, device_id_type=MESH)

    def xg_back(yt, d):
        return pltpu.make_async_remote_copy(
            src_ref=XG.at[xc, yt], dst_ref=XG.at[lax.rem(xc + 4 - d, 4), yt],
            send_sem=ss_c.at[yt, d - 1], recv_sem=rs_c.at[yt, d - 1],
            device_id={"gx": lax.rem(gx + 2 * d, 8)}, device_id_type=MESH)

    middles = []
    for yt in range(2):
        pair(yt).wait_recv()
        mine = [XOWN[yt, i] for i in range(5)]
        peer = [XPEER[yt, i] for i in range(5)]
        merged_x, middle = merge_blocks([jnp.where(low_x, a, b) for a, b in zip(mine, peer)],
                                        [jnp.where(low_x, b, a) for a, b in zip(mine, peer)])
        middles.append(middle)
        for i in range(5):
            XG[xc, yt, i] = merged_x[i]
        for d in (1, 2, 3):
            xg_copy(yt, d).start()
    middle_x = [jnp.stack(part) for part in zip(*middles)]

    middles_z = [merge_cores(half)[1] for half in range(2)]
    for half in range(2):
        for k in range(SOLVERS):
            @pl.when(jnp.logical_or(zc != FIRST_SOLVER + k, core != half))
            def _():
                from_solver(half, k).wait_recv()

    first_z, next_z = [], []
    for half in range(2):
        start, end = [jnp.stack([RV[pl.ds(4 * 8 * half + 2 * w + yt, 8, stride=4), :] for yt in range(2)])
                      for w in range(2)]
        to_l, to_r, source = middles_z[half]
        middle = source + to_l * start + to_r * end
        first_z.append(jnp.where(low, start, middle))
        next_z.append(jnp.where(low, middle, end))

    for yt in range(2):
        for d in (1, 2, 3):
            xg_back(yt, d).wait_recv()
    ground, source = XG[0, :, 1], XG[0, :, 3]
    stack = []
    for p in range(4):
        series = XG[p, :, 0]
        inverse = 1.0 / (ground + series)
        ratio = series * inverse
        stack.append((source * inverse, ratio))
        if p < 3:
            ground = XG[p + 1, :, 1] + XG[p, :, 2] + ratio * ground
            source = XG[p + 1, :, 3] + XG[p, :, 4] + ratio * source
    value = stack[3][0]
    SG[4] = jnp.zeros((2, 8, 128), F32)
    SG[3] = value
    for p in (2, 1, 0):
        value = stack[p][0] + stack[p][1] * value
        SG[p] = value
    start_x, end_x = SG[xc], SG[xc + 1]
    middle_node = middle_x[2] + middle_x[0] * start_x + middle_x[1] * end_x
    first = jnp.where(low_x, start_x, middle_node)
    end_own = jnp.where(low_x, middle_node, end_x)
    middle_block = middle_own[2] + middle_own[0] * first + middle_own[1] * end_own
    first, solved = jnp.stack([first, middle_block]), jnp.stack([middle_block, end_own])

    def add_x(j, value):
        for half in range(2):
            at = 64 * half + 8 * j
            for yt in range(2):
                XY[yt, at:at + 8, :] = XY[yt, at:at + 8, :] + value[half, yt]
    add_x(0, first)
    for j in range(7, 0, -1):
        solved = XA[2, j] + XA[0, j] * first + XA[1, j] * solved
        add_x(j, solved)

    first, solved = jnp.concatenate(first_z, axis=1), jnp.concatenate(next_z, axis=1)

    def write(j, value):
        for yt in range(2):
            o_ref[16 * j:16 * j + 16, 128 * yt:128 * yt + 128] = value[yt] + XY[yt, pl.ds(j, 16, stride=8), :]
    write(0, first)
    for j in range(7, 0, -1):
        solved = ZA[2, j] + ZA[0, j] * first + ZA[1, j] * solved
        write(j, solved)

    for i, yt in both:
        @pl.when(sends_x[i])
        def _():
            x_copy(i, yt).wait_send()
    near_send(0)
    near_send(1)
    for yt in range(2):
        pair(yt).wait_send()
        for d in (1, 2, 3):
            xg_copy(yt, d).wait_send()
    for d in (1, 2, 3):
        y_copy(d).wait_send()
    for k in range(SOLVERS):
        @pl.when(zc != FIRST_SOLVER + k)
        def _():
            to_solver(k).wait_send()

    @pl.when(is_solver)
    def _():
        for p in range(8):
            to_chip(p, 1).wait_send()

            @pl.when(zc != p)
            def _():
                to_chip(p, 0).wait_send()
    cores.wait_send()


def body(volume):
    tile = (8, 128)
    dma = pltpu.SemaphoreType.DMA
    vmem = [
        (128, 256),
        (3, 2, 27) + tile,
        (2, 2) + tile,
        (3, 2, 2) + tile,
        (27, 2, 3) + tile,
        (23, 2, 3) + tile,
        (3, 21, 2, 3) + tile,
        (17, 2) + tile,
        (2, 128, 128),
        (2, 128, 128),
        (3, 8, 2, 2) + tile,
        (2, 5) + tile,
        (2, 5) + tile,
        (4, 2, 5) + tile,
        (5, 2) + tile,
        (3, 8, 2, 16, 128),
        (2, 5, 2) + tile,
        (2, 5, 2) + tile,
        (80, 128),
        (8 * MESSAGE, 128),
        (8 * ANSWER, 128),
        (64, 128),
        (256, 128),
        (256, 128),
        (3, 32) + tile,
        (5,) + tile,
        (4, 5) + tile,
        (2, 4) + tile,
        (2, 128, 128),
    ]
    sems = [None, (2, 10), (2, 10), (2, 2), (2, 2), (2,), (2,), (2, 3), (2, 3), (3,), (3,), None, None, (SOLVERS,), (8,), (2, 8), (2 * SOLVERS,)]
    total = pl.pallas_call(
        kernel,
        out_shape=jax.ShapeDtypeStruct((128, 256), F32),
        in_specs=[pl.BlockSpec(memory_space=pltpu.HBM)],
        out_specs=pl.BlockSpec(memory_space=pltpu.VMEM),
        scratch_shapes=[pltpu.VMEM(shape, F32) for shape in vmem] + [dma(s) if s else dma for s in sems],
        compiler_params=pltpu.CompilerParams(
            collective_id=0, has_side_effects=True, vmem_limit_bytes=24 * 2**20),
        cost_estimate=pl.CostEstimate(flops=40_000_000, bytes_accessed=262144, transcendentals=0),
    )(volume.reshape(128, 256))
    return (total / 3.0).reshape(8, 16, 256)


def solution(mesh):
    return jax.shard_map(
        body,
        mesh=mesh,
        in_specs=(P("gz", "gx", "gy"),),
        out_specs=P("gz", "gx", "gy"),
        check_vma=False,
    )
```

```python
import functools

import jax
import jax.numpy as jnp
from jax import lax
from jax.experimental import pallas as pl
from jax.experimental.pallas import tpu as pltpu
from jax.sharding import PartitionSpec as P

MESH = pl.DeviceIdType.MESH
F32 = jnp.float32
RAW_TAPS = (0.41111229, 0.8007374, 1.0, 0.8007374, 0.41111229)
TAPS = tuple(tap / sum(RAW_TAPS) for tap in RAW_TAPS)
STIFFNESS = 9000.0
CONTRAST = 0.1
NEAR = tuple((dz, dy) for dz in (-1, 0, 1) for dy in (-1, 0, 1) if dz or dy)
NEAR_HALO = tuple((dz, dy, yt) for yt, dy_end in ((0, -1), (1, 1)) for dz in (-1, 0, 1) for dy in (0, dy_end) if dz or dy)
SOLVERS = 2
FIRST_SOLVER = 3
ROWS = 8 // SOLVERS
MESSAGE, ANSWER = 10 * ROWS, 4 * ROWS
U_BLUR, U_X, U_SLOPE, U_FACE = 4, 4, 5, 8


def roll_z(tile, j):
    return pltpu.roll(tile, (-j) % 8, tile.ndim - 2)


def roll_y(tile, j):
    return pltpu.roll(tile, (-j) % 128, tile.ndim - 1)


def taps_sum(parts):
    return TAPS[2] * parts[2] + TAPS[1] * (parts[1] + parts[3]) + TAPS[0] * (parts[0] + parts[4])


def ring_z(tiles, t, j, row):
    if j == 0:
        return tiles[t]
    if j > 0:
        return jnp.where(row < 8 - j, roll_z(tiles[t], j), roll_z(tiles[1 - t], j))
    return jnp.where(row >= -j, roll_z(tiles[t], j), roll_z(tiles[1 - t], j))


def ring_y(tiles, t, j, lane):
    if j == 0:
        return tiles[t]
    if j > 0:
        return jnp.where(lane < 128 - j, roll_y(tiles[t], j), roll_y(tiles[(t + 1) % 3], j))
    return jnp.where(lane >= -j, roll_y(tiles[t], j), roll_y(tiles[(t + 2) % 3], j))


def wide_z(down, own, up, row):
    inner, outer = [], []
    for j in range(-2, 3):
        if j == 0:
            inner.append(own)
            outer.append(jnp.where(row < 4, up, down))
            continue
        down_j, own_j, up_j = roll_z(down, j), roll_z(own, j), roll_z(up, j)
        if j > 0:
            inner.append(jnp.where(row < 8 - j, own_j, up_j))
            outer.append(jnp.where(row < 4, up_j, jnp.where(row < 8 - j, down_j, own_j)))
        else:
            inner.append(jnp.where(row >= -j, own_j, down_j))
            outer.append(jnp.where(row >= 4, down_j, jnp.where(row >= -j, up_j, own_j)))
    return taps_sum(inner), taps_sum(outer)


def loop(first, last, step, unroll):
    trips = (last - first) // unroll

    def some(t, carry):
        for u in range(unroll):
            step(first + t * unroll + u)
        return carry
    if trips:
        lax.fori_loop(0, trips, some, 0)
    for i in range(first + trips * unroll, last):
        step(i)


def reciprocal(value):
    guess = pl.reciprocal(value, approx=True)
    for _ in range(1):
        guess = guess * (2.0 - value * guess)
    return guess


def reduce_block(count, get_face, get_value, keep):
    series = get_face(0)
    left_ground = jnp.ones_like(series)
    left_source = get_value(0)
    ground = jnp.ones_like(series)
    source = get_value(1)
    for j in range(1, count):
        face = get_face(j)
        inverse = reciprocal(series + ground + face)
        to_left, to_next = series * inverse, face * inverse
        keep(j, to_left, to_next, source * inverse)
        left_ground = left_ground + to_left * ground
        left_source = left_source + to_left * source
        series = to_left * face
        if j < count - 1:
            ground = 1.0 + to_next * ground
            source = get_value(j + 1) + to_next * source
    return series, left_ground, to_next * ground, left_source, to_next * source


def merge_blocks(left, right):
    a_l, gl_l, gr_l, il_l, ir_l = left
    a_r, gl_r, gr_r, il_r, ir_r = right
    ground, source = gr_l + gl_r, ir_l + il_r
    inverse = reciprocal(a_l + ground + a_r)
    to_l, to_r = a_l * inverse, a_r * inverse
    merged = (to_l * a_r, gl_l + to_l * ground, gr_r + to_r * ground, il_l + to_l * source, ir_r + to_r * source)
    return merged, (to_l, to_r, source * inverse)


def ladder_rings(series, ground, source, count, axis):
    size = series.shape[axis]
    step = 1
    while step < count:
        def low(array):
            return pltpu.roll(array, step, axis)

        def high(array):
            return pltpu.roll(array, size - step, axis)

        before = low(series)
        inverse = reciprocal(ground + series + before)
        from_low, from_high = before * low(inverse), series * high(inverse)
        ground, source, series = (
            ground + from_low * low(ground) + from_high * high(ground),
            source + from_low * low(source) + from_high * high(source),
            from_high * high(series),
        )
        step *= 2
    return source * reciprocal(ground)


def kernel(v_hbm, o_ref, v_ref, B, HS, HB, C, BL, SQ, GX, GZ, GY, XA, XOWN, XPEER, XG, SG, ZA, PZ, ZPEER,
           MS, ZR, RT, RV, GT, VT, YA, PY, YG, YS, XY, in_sem, ss_h, rs_h, ss_x, rs_x, ss_p, rs_p,
           ss_c, rs_c, ss_y, rs_y, ss_k, rs_k, ss_a, rs_a, ss_r, rs_r):
    gx, gy, gz = lax.axis_index("gx"), lax.axis_index("gy"), lax.axis_index("gz")
    zc, core = lax.div(gz, 2), lax.rem(gz, 2)
    xc, zh = lax.div(gx, 2), lax.rem(gx, 2)
    other_core = gz + 1 - 2 * core
    load = pltpu.make_async_copy(v_hbm, v_ref, in_sem)
    load.start()

    row = lax.broadcasted_iota(jnp.int32, (8, 128), 0)
    lane = lax.broadcasted_iota(jnp.int32, (8, 128), 1)

    def inside(dz, dy):
        z, y = gz + dz, gy + dy
        return jnp.logical_and(jnp.logical_and(z >= 0, z < 16), jnp.logical_and(y >= 0, y < 4))

    barrier = pltpu.get_barrier_semaphore()
    always = []
    for d in (2, 4, 6):
        always.append({"gx": lax.rem(gx + d, 8)})
    for d in (1, 2, 3):
        always.append({"gy": lax.rem(gy + d, 4)})
    is_solver = jnp.logical_and(zc >= FIRST_SOLVER, zc < FIRST_SOLVER + SOLVERS)
    total = jnp.int32(len(always))

    @pl.when(gx > 0)
    def _():
        pl.semaphore_signal(barrier, inc=1, device_id={"gx": gx - 1}, device_id_type=MESH)

    @pl.when(gx < 7)
    def _():
        pl.semaphore_signal(barrier, inc=1, device_id={"gx": gx + 1}, device_id_type=MESH)

    total = total + jnp.where(gx > 0, 1, 0) + jnp.where(gx < 7, 1, 0)
    for target in always:
        pl.semaphore_signal(barrier, inc=1, device_id=target, device_id_type=MESH)
    for p in range(8):
        solves = FIRST_SOLVER <= p < FIRST_SOLVER + SOLVERS
        meets = zc != p if solves else is_solver
        total = total + jnp.where(meets, 1, 0)

        @pl.when(meets)
        def _():
            pl.semaphore_signal(barrier, inc=1, device_id={"gz": 2 * p + core}, device_id_type=MESH)
    for dz, dy in NEAR:
        total = total + jnp.where(inside(dz, dy), 1, 0)

        @pl.when(inside(dz, dy))
        def _():
            pl.semaphore_signal(barrier, inc=1, device_id={"gz": gz + dz, "gy": gy + dy}, device_id_type=MESH)

    def pack(phase, layers, yt):
        packed = None
        for i, x in enumerate(layers):
            shift = (8 * i + 8 * yt) % 128
            tile = pltpu.roll(B[1, yt, x], shift, 1) if shift else B[1, yt, x]
            packed = tile if packed is None else jnp.where(lane < 8 * i, packed, tile)
        HS[yt, phase] = packed

    load.wait()
    for yt in range(2):
        XY[yt] = v_ref[:, 128 * yt:128 * yt + 128]
    for x in range(16):
        for yt in range(2):
            B[1, yt, x] = XY[yt, pl.ds(x, 8, stride=16), :]
    pack(0, range(16), 0)
    pack(0, range(16), 1)

    @pl.when(gz == 0)
    def _():
        B[0] = jnp.zeros((2, 27, 8, 128), F32)
        HB[0] = jnp.zeros((2, 2, 8, 128), F32)

    @pl.when(gz == 15)
    def _():
        B[2] = jnp.zeros((2, 27, 8, 128), F32)
        HB[2] = jnp.zeros((2, 2, 8, 128), F32)

    @pl.when(gy == 0)
    def _():
        for zt in range(3):
            HB[zt, 0] = jnp.zeros((2, 8, 128), F32)

    @pl.when(gy == 3)
    def _():
        for zt in range(3):
            HB[zt, 1] = jnp.zeros((2, 8, 128), F32)

    @pl.when(gx == 0)
    def _():
        for yt in range(2):
            B[1, yt, 22:27] = jnp.zeros((5, 8, 128), F32)

    @pl.when(gx == 7)
    def _():
        for yt in range(2):
            B[1, yt, 16:22] = jnp.zeros((6, 8, 128), F32)

    pl.semaphore_wait(barrier, total)

    def x_copy(i, yt):
        source, target, device = ((B.at[1, yt, 0:6], B.at[1, yt, 16:22], {"gx": gx - 1}),
                                  (B.at[1, yt, 11:16], B.at[1, yt, 22:27], {"gx": gx + 1}))[i]
        return pltpu.make_async_remote_copy(
            src_ref=source, dst_ref=target, send_sem=ss_x.at[i, yt], recv_sem=rs_x.at[i, yt],
            device_id=device, device_id_type=MESH)

    sends_x = (gx > 0, gx < 7)
    gets_x = (gx < 7, gx > 0)
    both = [(i, yt) for yt in range(2) for i in range(2)]

    for i, yt in both:
        @pl.when(sends_x[i])
        def _():
            x_copy(i, yt).start()

    def near_copy(phase, i):
        if phase == 0:
            dz, dy = NEAR[i]
            ys, xs = slice(0, 2), slice(0, 16)
        else:
            dz, dy, yt = NEAR_HALO[i]
            ys, xs = yt, slice(16, 27)
        if dy == 0:
            source, target = B.at[1, ys, xs], B.at[1 - dz, ys, xs]
        elif dy == 1:
            source, target = HS.at[1, phase], HB.at[1 - dz, 0, phase]
        else:
            source, target = HS.at[0, phase], HB.at[1 - dz, 1, phase]
        return pltpu.make_async_remote_copy(
            src_ref=source, dst_ref=target, send_sem=ss_h.at[phase, i], recv_sem=rs_h.at[phase, i],
            device_id={"gz": gz + dz, "gy": gy + dy}, device_id_type=MESH)

    def near_list(phase):
        return [d[:2] for d in (NEAR, NEAR_HALO)[phase]]

    def near_start(phase, first, last):
        for i, (dz, dy) in enumerate(near_list(phase)):
            if first <= i < last:
                @pl.when(inside(dz, dy))
                def _():
                    near_copy(phase, i).start()

    def near_recv(phase):
        for i, (dz, dy) in enumerate(near_list(phase)):
            @pl.when(inside(-dz, -dy))
            def _():
                near_copy(phase, i).wait_recv()

    def near_send(phase):
        for i, (dz, dy) in enumerate(near_list(phase)):
            @pl.when(inside(dz, dy))
            def _():
                near_copy(phase, i).wait_send()

    near_start(0, 0, 8)

    def blur_zy(xi, phase):
        columns = []
        layer = xi - 16 * phase
        to_low, to_high = lax.rem(128 - 8 * layer, 128), 120 - 8 * layer
        for zt in range(3):
            halo = jnp.where(lane < 64, pltpu.roll(HB[zt, 1, phase], to_low, 1), pltpu.roll(HB[zt, 0, phase], to_high, 1))
            columns.append([B[zt, 0, xi], B[zt, 1, xi], halo])
        inner, outer = [], []
        for yt in range(3):
            a, b = wide_z(columns[0][yt], columns[1][yt], columns[2][yt], row)
            inner.append(a)
            outer.append(b)
        place = lax.rem(xi + 5, 27)
        for zt, tiles in enumerate((inner, outer)):
            for yt in range(3):
                C[place, zt, yt] = taps_sum([ring_y(tiles, yt, j, lane) for j in range(-2, 3)])

    def blur_x(p):
        for zt in range(2):
            for yt in range(3):
                BL[p, zt, yt] = taps_sum([C[p + j, zt, yt] for j in range(5)])

    above = jnp.where(gz < 15, 0.5, 0.0)
    below = jnp.where(gz > 0, 0.5, 0.0)
    right = jnp.where(gy < 3, 1.0, 0.0)
    left = jnp.where(gy > 0, 1.0, 0.0)
    z_half = (jnp.full((8, 128), 0.5, F32), jnp.where(row < 4, above, below).astype(F32))
    y_one = jnp.where(lane < 64, right, left).astype(F32)
    halves = [[z_half[0], z_half[0], z_half[0] * y_one], [z_half[1], z_half[1], z_half[1] * y_one]]

    def slopes(p, axes):
        x_in = jnp.where(jnp.logical_or(jnp.logical_and(p < 2, gx == 0), jnp.logical_and(p > 17, gx == 7)), 0.0, 1.0)
        tiles = [[BL[p + 1, zt, yt] for yt in range(3)] for zt in range(2)]
        for zt in range(2):
            for yt in range(3):
                half = halves[zt][yt] * x_in
                for axis in axes:
                    if axis == 0:
                        change = BL[p + 2, zt, yt] - BL[p, zt, yt]
                    elif axis == 1:
                        column = [tiles[0][yt], tiles[1][yt]]
                        change = ring_z(column, zt, 1, row) - ring_z(column, zt, -1, row)
                    else:
                        change = ring_y(tiles[zt], yt, 1, lane) - ring_y(tiles[zt], yt, -1, lane)
                    slope = change * half
                    SQ[axis, p, zt, yt] = slope * slope

    def outer_slopes(axis):
        loop(0, 5, lambda p: slopes(p, (axis,)), 5)
        loop(15, 21, lambda p: slopes(p, (axis,)), 6)

    near_recv(0)
    loop(0, 16, lambda xi: blur_zy(xi, 0), U_BLUR)
    loop(5, 17, blur_x, U_X)
    loop(5, 15, lambda p: slopes(p, (0, 1, 2)), U_SLOPE)

    for yt in range(2):
        for i in range(2):
            @pl.when(gets_x[i])
            def _():
                x_copy(i, yt).wait_recv()
        pack(1, range(16, 27), yt)
        near_start(1, 5 * yt, 5 * yt + 5)
    near_recv(1)
    loop(16, 27, lambda xi: blur_zy(xi, 1), U_BLUR)
    loop(0, 5, blur_x, U_X)
    loop(17, 23, blur_x, U_X)
    outer_slopes(0)

    def diffuse(tensor):
        return reciprocal(1.0 + tensor * (1.0 / (CONTRAST * CONTRAST)))

    def tensor_x(a, p):
        return [[taps_sum([SQ[a, p + j, zt, yt] for j in range(5)]) for yt in range(3)] for zt in range(2)]

    def tensor_z(tiles, zt):
        return [taps_sum([ring_z([tiles[0][yt], tiles[1][yt]], zt, j, row) for j in range(-2, 3)]) for yt in range(3)]

    def tensor_y(tiles, yt):
        return taps_sum([ring_y(tiles, yt, j, lane) for j in range(-2, 3)])

    def face_x(p):
        tiles = tensor_z(tensor_x(0, p), 0)
        for yt in range(2):
            GX[p, yt] = diffuse(tensor_y(tiles, yt))
    loop(0, 17, face_x, U_FACE)
    last_x = jnp.where(gx == 7, 0.0, 0.5 * STIFFNESS)

    def get_gx(j):
        return (GX[j] + GX[j + 1]) * (last_x if j == 15 else 0.5 * STIFFNESS)

    def keep_x(j, to_left, to_next, source):
        XA[0, j], XA[1, j], XA[2, j] = to_left, to_next, source

    def halves_of(get):
        return lambda j: jnp.stack([get(j), get(j + 8)])

    halved = reduce_block(8, halves_of(get_gx), halves_of(lambda j: B[1, :, j]), keep_x)
    own_x, middle_own = merge_blocks([part[0] for part in halved], [part[1] for part in halved])
    for i in range(5):
        for yt in range(2):
            XOWN[yt, i] = own_x[i][yt]

    def pair(yt):
        return pltpu.make_async_remote_copy(
            src_ref=XOWN.at[yt], dst_ref=XPEER.at[yt], send_sem=ss_p.at[yt], recv_sem=rs_p.at[yt],
            device_id={"gx": gx + 1 - 2 * zh}, device_id_type=MESH)

    for yt in range(2):
        pair(yt).start()

    z_scale = jnp.where(jnp.logical_and(row == 7, gz == 15), 0.0, 0.5 * STIFFNESS).astype(F32)

    def face_z(p):
        tiles = tensor_x(1, p)
        rows = [tensor_z(tiles, zt) for zt in range(2)]
        at = p * 8 if isinstance(p, int) else pl.multiple_of(p * 8, 8)
        for yt in range(2):
            own, halo = diffuse(tensor_y(rows[0], yt)), diffuse(tensor_y(rows[1], yt))
            GZ[yt, pl.ds(at, 8), :] = (own + ring_z([own, halo], 0, 1, row)) * z_scale
    outer_slopes(1)
    loop(0, 16, face_z, U_FACE)

    def keep_z(j, to_left, to_next, source):
        ZA[0, j], ZA[1, j], ZA[2, j] = to_left, to_next, source

    def get_gz(j):
        return jnp.stack([GZ[yt, pl.ds(j, 16, stride=8), :] for yt in range(2)])

    def get_vz(j):
        return jnp.stack([v_ref[16 * j:16 * j + 16, 128 * yt:128 * yt + 128] for yt in range(2)])

    own_z = reduce_block(8, get_gz, get_vz, keep_z)
    for i in range(5):
        for h in range(2):
            PZ[h, i] = own_z[i][:, 8 * h:8 * h + 8, :]
    cores = pltpu.make_async_remote_copy(
        src_ref=PZ, dst_ref=ZPEER, send_sem=ss_k, recv_sem=rs_k,
        device_id={"gz": other_core}, device_id_type=MESH)
    cores.start()

    y_scale = (jnp.full((8, 128), 0.5 * STIFFNESS, F32),
               jnp.where(jnp.logical_and(lane == 127, gy == 3), 0.0, 0.5 * STIFFNESS).astype(F32))

    def face_y(p):
        tiles = tensor_z(tensor_x(2, p), 0)
        values = [diffuse(tensor_y(tiles, yt)) for yt in range(3)]
        at = p * 8 if isinstance(p, int) else pl.multiple_of(p * 8, 8)
        for yt in range(2):
            GY[yt, pl.ds(at, 8), :] = (values[yt] + ring_y(values, yt, 1, lane)) * y_scale[yt]
    outer_slopes(2)
    loop(0, 16, face_y, U_FACE)

    cores.wait_recv()
    low = core == 0

    def merge_cores(half):
        mine = [PZ[half, i] for i in range(5)]
        peer = [ZPEER[half, i] for i in range(5)]
        return merge_blocks([jnp.where(low, a, b) for a, b in zip(mine, peer)],
                            [jnp.where(low, b, a) for a, b in zip(mine, peer)])

    merged_z = merge_cores(core)[0]
    for i in range(5):
        for yt in range(2):
            MS[pl.ds(2 * i + yt, 8, stride=10), :] = merged_z[i][yt]

    def to_solver(k):
        return pltpu.make_async_remote_copy(
            src_ref=MS.at[pl.ds(MESSAGE * k, MESSAGE)],
            dst_ref=ZR.at[pl.ds(pl.multiple_of(zc * MESSAGE, 8), MESSAGE)],
            send_sem=ss_a.at[k], recv_sem=rs_a.at[zc],
            device_id={"gz": 2 * (FIRST_SOLVER + k) + core}, device_id_type=MESH)

    def from_chip(p):
        return pltpu.make_async_remote_copy(
            src_ref=MS.at[pl.ds(0, MESSAGE)], dst_ref=ZR.at[pl.ds(MESSAGE * p, MESSAGE)],
            send_sem=ss_a.at[0], recv_sem=rs_a.at[p],
            device_id={"gz": other_core}, device_id_type=MESH)

    for k in range(SOLVERS):
        @pl.when(zc != FIRST_SOLVER + k)
        def _():
            to_solver(k).start()

        @pl.when(zc == FIRST_SOLVER + k)
        def _():
            place = MESSAGE * (FIRST_SOLVER + k)
            ZR[place:place + MESSAGE, :] = MS[MESSAGE * k:MESSAGE * k + MESSAGE, :]

    for yt in range(2):
        GT[128 * yt:128 * yt + 128, :] = GY[yt].T
        VT[128 * yt:128 * yt + 128, :] = B[1, yt, 0:16].reshape(128, 128).T

    def keep_y(j, to_left, to_next, source):
        YA[0, j], YA[1, j], YA[2, j] = to_left, to_next, source

    own_y = reduce_block(32, lambda j: GT[pl.ds(j, 8, stride=32), :], lambda j: VT[pl.ds(j, 8, stride=32), :], keep_y)
    for i in range(5):
        PY[i] = own_y[i]

    def y_copy(d):
        return pltpu.make_async_remote_copy(
            src_ref=PY, dst_ref=YG.at[gy], send_sem=ss_y.at[d - 1], recv_sem=rs_y.at[d - 1],
            device_id={"gy": lax.rem(gy + d, 4)}, device_id_type=MESH)

    def y_back(d):
        return pltpu.make_async_remote_copy(
            src_ref=PY, dst_ref=YG.at[lax.rem(gy + 4 - d, 4)], send_sem=ss_y.at[d - 1], recv_sem=rs_y.at[d - 1],
            device_id={"gy": lax.rem(gy + d, 4)}, device_id_type=MESH)

    for d in (1, 2, 3):
        y_copy(d).start()
    YG[gy] = PY[...]

    place = jnp.clip(zc - FIRST_SOLVER, 0, SOLVERS - 1)

    def to_chip(p, side):
        return pltpu.make_async_remote_copy(
            src_ref=RT.at[pl.ds(ANSWER * p, ANSWER)],
            dst_ref=RV.at[pl.ds(pl.multiple_of((core * SOLVERS + place) * ANSWER, 8), ANSWER)],
            send_sem=ss_r.at[side, p], recv_sem=rs_r.at[core * SOLVERS + place],
            device_id={"gz": 2 * p + (1 - core if side else core)}, device_id_type=MESH)

    def from_solver(half, k):
        at = half * SOLVERS + k
        return pltpu.make_async_remote_copy(
            src_ref=RT.at[pl.ds(0, ANSWER)], dst_ref=RV.at[pl.ds(ANSWER * at, ANSWER)],
            send_sem=ss_r.at[0, 0], recv_sem=rs_r.at[at],
            device_id={"gz": other_core}, device_id_type=MESH)

    far_first = sorted(range(8), key=lambda p: -abs(2 * p - 7))

    @pl.when(is_solver)
    def _():
        for p in range(8):
            @pl.when(zc != p)
            def _():
                from_chip(p).wait_recv()

        def gather(i):
            return jnp.stack([ZR[pl.ds(10 * rr + 2 * i + yt, 8, stride=MESSAGE), :] for rr in range(ROWS) for yt in range(2)])
        series, gl, gr, il, ir = [gather(i) for i in range(5)]
        sigma = ladder_rings(series, gl + pltpu.roll(gr, 1, 1), il + pltpu.roll(ir, 1, 1), 8, 1)
        following = pltpu.roll(sigma, 7, 1)
        for rr in range(ROWS):
            for yt in range(2):
                RT[pl.ds(4 * rr + yt, 8, stride=ANSWER), :] = sigma[2 * rr + yt]
                RT[pl.ds(4 * rr + 2 + yt, 8, stride=ANSWER), :] = following[2 * rr + yt]
        for p in far_first:
            to_chip(p, 1).start()

            @pl.when(zc != p)
            def _():
                to_chip(p, 0).start()

            @pl.when(zc == p)
            def _():
                at = pl.multiple_of((core * SOLVERS + place) * ANSWER, 8)
                RV[pl.ds(at, ANSWER), :] = RT[ANSWER * p:ANSWER * p + ANSWER, :]

    low_x = zh == 0

    def xg_copy(yt, d):
        return pltpu.make_async_remote_copy(
            src_ref=XG.at[xc, yt], dst_ref=XG.at[xc, yt], send_sem=ss_c.at[yt, d - 1], recv_sem=rs_c.at[yt, d - 1],
            device_id={"gx": lax.rem(gx + 2 * d, 8)}, device_id_type=MESH)

    def xg_back(yt, d):
        return pltpu.make_async_remote_copy(
            src_ref=XG.at[xc, yt], dst_ref=XG.at[lax.rem(xc + 4 - d, 4), yt],
            send_sem=ss_c.at[yt, d - 1], recv_sem=rs_c.at[yt, d - 1],
            device_id={"gx": lax.rem(gx + 2 * d, 8)}, device_id_type=MESH)

    middles = []
    for yt in range(2):
        pair(yt).wait_recv()
        mine = [XOWN[yt, i] for i in range(5)]
        peer = [XPEER[yt, i] for i in range(5)]
        merged_x, middle = merge_blocks([jnp.where(low_x, a, b) for a, b in zip(mine, peer)],
                                        [jnp.where(low_x, b, a) for a, b in zip(mine, peer)])
        middles.append(middle)
        for i in range(5):
            XG[xc, yt, i] = merged_x[i]
        for d in (2, 1, 3):
            xg_copy(yt, d).start()
    middle_x = [jnp.stack(part) for part in zip(*middles)]

    for d in (1, 2, 3):
        y_back(d).wait_recv()
    series, gl, gr, il, ir = [YG[:, i].reshape(32, 128) for i in range(5)]
    sigma = ladder_rings(series, gl + pltpu.roll(gr, 1, 0), il + pltpu.roll(ir, 1, 0), 32, 0)
    YS[0] = sigma.reshape(4, 8, 128)
    YS[1] = pltpu.roll(sigma, 31, 0).reshape(4, 8, 128)
    first, solved = YS[0, gy], YS[1, gy]
    VT[pl.ds(0, 8, stride=32), :] = first
    for j in range(31, 0, -1):
        solved = YA[2, j] + YA[0, j] * first + YA[1, j] * solved
        VT[pl.ds(j, 8, stride=32), :] = solved
    for yt in range(2):
        XY[yt] = VT[128 * yt:128 * yt + 128, :].T

    middles_z = [merge_cores(half)[1] for half in range(2)]
    for half in range(2):
        for k in range(SOLVERS):
            @pl.when(jnp.logical_or(zc != FIRST_SOLVER + k, core != half))
            def _():
                from_solver(half, k).wait_recv()

    first_z, next_z = [], []
    for half in range(2):
        start, end = [jnp.stack([RV[pl.ds(4 * 8 * half + 2 * w + yt, 8, stride=4), :] for yt in range(2)])
                      for w in range(2)]
        to_l, to_r, source = middles_z[half]
        middle = source + to_l * start + to_r * end
        first_z.append(jnp.where(low, start, middle))
        next_z.append(jnp.where(low, middle, end))

    for yt in range(2):
        for d in (1, 2, 3):
            xg_back(yt, d).wait_recv()
    ground, source = XG[0, :, 1], XG[0, :, 3]
    stack = []
    for p in range(4):
        series = XG[p, :, 0]
        inverse = reciprocal(ground + series)
        ratio = series * inverse
        stack.append((source * inverse, ratio))
        if p < 3:
            ground = XG[p + 1, :, 1] + XG[p, :, 2] + ratio * ground
            source = XG[p + 1, :, 3] + XG[p, :, 4] + ratio * source
    value = stack[3][0]
    SG[4] = jnp.zeros((2, 8, 128), F32)
    SG[3] = value
    for p in (2, 1, 0):
        value = stack[p][0] + stack[p][1] * value
        SG[p] = value
    start_x, end_x = SG[xc], SG[xc + 1]
    middle_node = middle_x[2] + middle_x[0] * start_x + middle_x[1] * end_x
    first = jnp.where(low_x, start_x, middle_node)
    end_own = jnp.where(low_x, middle_node, end_x)
    middle_block = middle_own[2] + middle_own[0] * first + middle_own[1] * end_own
    first, solved = jnp.stack([first, middle_block]), jnp.stack([middle_block, end_own])

    def add_x(j, value):
        for half in range(2):
            at = 64 * half + 8 * j
            for yt in range(2):
                XY[yt, at:at + 8, :] = XY[yt, at:at + 8, :] + value[half, yt]
    add_x(0, first)
    for j in range(7, 0, -1):
        solved = XA[2, j] + XA[0, j] * first + XA[1, j] * solved
        add_x(j, solved)

    first, solved = jnp.concatenate(first_z, axis=1), jnp.concatenate(next_z, axis=1)

    def write(j, value):
        for yt in range(2):
            o_ref[16 * j:16 * j + 16, 128 * yt:128 * yt + 128] = value[yt] + XY[yt, pl.ds(j, 16, stride=8), :]
    write(0, first)
    for j in range(7, 0, -1):
        solved = ZA[2, j] + ZA[0, j] * first + ZA[1, j] * solved
        write(j, solved)

    for i, yt in both:
        @pl.when(sends_x[i])
        def _():
            x_copy(i, yt).wait_send()
    near_send(0)
    near_send(1)
    for yt in range(2):
        pair(yt).wait_send()
        for d in (1, 2, 3):
            xg_copy(yt, d).wait_send()
    for d in (1, 2, 3):
        y_copy(d).wait_send()
    for k in range(SOLVERS):
        @pl.when(zc != FIRST_SOLVER + k)
        def _():
            to_solver(k).wait_send()

    @pl.when(is_solver)
    def _():
        for p in range(8):
            to_chip(p, 1).wait_send()

            @pl.when(zc != p)
            def _():
                to_chip(p, 0).wait_send()
    cores.wait_send()


def body(volume):
    tile = (8, 128)
    dma = pltpu.SemaphoreType.DMA
    vmem = [
        (128, 256),
        (3, 2, 27) + tile,
        (2, 2) + tile,
        (3, 2, 2) + tile,
        (27, 2, 3) + tile,
        (23, 2, 3) + tile,
        (3, 21, 2, 3) + tile,
        (17, 2) + tile,
        (2, 128, 128),
        (2, 128, 128),
        (3, 8, 2, 2) + tile,
        (2, 5) + tile,
        (2, 5) + tile,
        (4, 2, 5) + tile,
        (5, 2) + tile,
        (3, 8, 2, 16, 128),
        (2, 5, 2) + tile,
        (2, 5, 2) + tile,
        (80, 128),
        (8 * MESSAGE, 128),
        (8 * ANSWER, 128),
        (64, 128),
        (256, 128),
        (256, 128),
        (3, 32) + tile,
        (5,) + tile,
        (4, 5) + tile,
        (2, 4) + tile,
        (2, 128, 128),
    ]
    sems = [None, (2, 10), (2, 10), (2, 2), (2, 2), (2,), (2,), (2, 3), (2, 3), (3,), (3,), None, None, (SOLVERS,), (8,), (2, 8), (2 * SOLVERS,)]
    total = pl.pallas_call(
        kernel,
        out_shape=jax.ShapeDtypeStruct((128, 256), F32),
        in_specs=[pl.BlockSpec(memory_space=pltpu.HBM)],
        out_specs=pl.BlockSpec(memory_space=pltpu.VMEM),
        scratch_shapes=[pltpu.VMEM(shape, F32) for shape in vmem] + [dma(s) if s else dma for s in sems],
        compiler_params=pltpu.CompilerParams(
            collective_id=0, has_side_effects=True, vmem_limit_bytes=24 * 2**20),
        cost_estimate=pl.CostEstimate(flops=40_000_000, bytes_accessed=262144, transcendentals=0),
    )(volume.reshape(128, 256))
    return (total / 3.0).reshape(8, 16, 256)


def solution(mesh):
    return jax.shard_map(
        body,
        mesh=mesh,
        in_specs=(P("gz", "gx", "gy"),),
        out_specs=P("gz", "gx", "gy"),
        check_vma=False,
    )
```
